32 devices in a mesh: row: 8 (over y, x, core), col: 4 (over z).
Axes of the slice: x: 2, y: 2, z: 4, core: 2. Of those that a mesh axis runs over, the one named last changes fastest.
Arguments:
- owned_rows: bfloat16 [768, 8192], P(('row', 'col')), may hold values from -6 to 6
- suffix_lengths: int32 [32], replicated, may hold values from 1 to 24, 256 in all
- owner_map: int32 [32], replicated, may hold values from 0 to 31, each once
- prefix_lengths: int32 [32], replicated, may hold values from 0 to 4095
- gate_weight: bfloat16 [8192, 29568], P('row', 'col'), may hold values from -0.0625 to 0.0625
- up_weight: bfloat16 [8192, 29568], P('row', 'col'), may hold values from -0.0625 to 0.0625
- down_weight: bfloat16 [29568, 8192], P('col', 'row'), may hold values from -0.03125 to 0.03125
Outputs:
- mixed: bfloat16 [256, 8192], P('col', 'row')
The draws below stay inside these ranges and needn't reach their ends.
Inputs may be any that keep to these rules, and one draw needn't show every extreme that they name: `suffix_lengths`: the lengths add up to 256; the largest is exactly 24. `owner_map`: each device owns one request; request r's suffix rows fill, in order, the first suffix_lengths[r] of the 24 slots of its owner in owned_rows, and the other slots are not used.
All inputs are finite; a program needn't handle non-finite values.
Results may differ from the reference program's by a relative error of at most 0.0049.
Values may be sent and summed in bfloat16 or wider, within the bound.
A program may use at most 128 MiB of HBM per device.

```python
import math
import jax
import jax.numpy as jnp
import numpy as np

D = 8192
FF = 29568
PREFIX_MAX = 4096
REQS = 32
TOKENS = 256
MOST = 24


def draw_prefix_lengths(key, part):
    base_key, pick_key = jax.random.split(jax.random.fold_in(key, 7))
    drawn_lengths = jax.random.randint(base_key, (REQS,), 0, PREFIX_MAX, dtype=jnp.int32)
    chosen = jax.random.permutation(pick_key, REQS)
    drawn_lengths = drawn_lengths.at[chosen[0]].set(PREFIX_MAX - 1)
    return drawn_lengths.at[chosen[1]].set(0)


def level_of(key, extent, pieces, least, largest):
    factor_of = 1.0
    for dim, parts in pieces:
        steps = jax.random.uniform(jax.random.fold_in(jax.random.fold_in(key, 6), dim), (parts,), jnp.float32, least / len(pieces), largest / len(pieces))
        factor_of = factor_of * jnp.repeat(jnp.exp(steps), extent[dim] // parts).reshape((-1,) + (1,) * (len(extent) - 1 - dim))
    return factor_of


def split_up(number_of, total, bound, slope):
    portions = [(1 << 20) // math.isqrt(rank ** slope) + 1 for rank in range(2, number_of + 1)]
    surplus, counts = total - bound - (number_of - 1), [1] * (number_of - 1)
    while surplus > 0:
        movable = [i for i in range(number_of - 1) if counts[i] < bound]
        mass, left = sum([portions[i] for i in movable]), surplus
        for i in movable:
            more = min(bound - counts[i], max(1, left * portions[i] // mass), surplus)
            counts[i] = counts[i] + more
            surplus = surplus - more
    return np.array([bound] + counts)


def uneven_parts(rng, count, total, limit, skew):
    if count == 2:
        one = jax.random.randint(rng, (), max(1, total - limit), min(limit, total - 1) + 1)
        return jnp.stack([one, total - one])
    sizes = jnp.asarray(split_up(count, total, limit, skew), jnp.int32)
    couples = (count - 1) // 2
    donor, sink = sizes[1:1 + 2 * couples:2], sizes[2:2 + 2 * couples:2]
    room = jnp.minimum(donor - 1, limit - sink)
    moved = jax.random.randint(jax.random.fold_in(rng, 1), (couples,), 0, 1 << 20) % (room + 1)
    sizes = sizes.at[1:1 + 2 * couples:2].set(donor - moved).at[2:2 + 2 * couples:2].set(sink + moved)
    return sizes[jax.random.permutation(jax.random.fold_in(rng, 2), count)]


def gaussian(key, shape, scale, most, pieces=(), held_as=jnp.bfloat16):
    array = scale * jax.random.normal(key, shape, jnp.float32)
    if pieces:
        array = array * level_of(key, shape, pieces, -0.22, 0.18)
    return jnp.clip(array, -most, most).astype(held_as)


def setup_inputs(seed: int = 0) -> dict:
    arg_keys = jax.random.split(jax.random.key(seed), 8)
    return {
        "owned_rows": gaussian(arg_keys[0], (REQS * MOST, D), 1.0, 6.0, ((0, 32),)),
        "suffix_lengths": uneven_parts(arg_keys[1], REQS, TOKENS, MOST, 2).astype(jnp.int32),
        "owner_map": jax.random.permutation(arg_keys[2], REQS).astype(jnp.int32),
        "prefix_lengths": draw_prefix_lengths(jax.random.fold_in(arg_keys[7], 71), 0),
        "gate_weight": gaussian(arg_keys[4], (D, FF), D ** -0.5, 0.0625, ((0, 8), (1, 4))),
        "up_weight": gaussian(arg_keys[5], (D, FF), D ** -0.5, 0.0625, ((0, 8), (1, 4))),
        "down_weight": gaussian(arg_keys[6], (FF, D), FF ** -0.5, 0.03125, ((0, 4), (1, 8))),
    }


def source_rows(suffix_lengths, owner_map, prefix_lengths, row_count, slot_size):
    request_ids = jnp.arange(suffix_lengths.shape[0], dtype=jnp.int32)
    longer = prefix_lengths[None, :] > prefix_lengths[:, None]
    earlier = (prefix_lengths[None, :] == prefix_lengths[:, None]) & (request_ids[None, :] < request_ids[:, None])
    starts = jnp.sum(jnp.where(longer | earlier, suffix_lengths[None, :], 0), axis=1).astype(jnp.int32)
    positions = jnp.arange(row_count, dtype=jnp.int32)
    ends = (starts + suffix_lengths).astype(jnp.int32)
    inside = (positions[:, None] >= starts[None, :]) & (positions[:, None] < ends[None, :])
    offsets = (owner_map * slot_size - starts).astype(jnp.int32)
    shifted = jnp.sum(jnp.where(inside, offsets[None, :], 0), axis=1).astype(jnp.int32)
    return (positions + shifted).astype(jnp.int32)


def reference(owned_rows, suffix_lengths, owner_map, prefix_lengths, gate_weight, up_weight, down_weight):
    source = source_rows(suffix_lengths, owner_map, prefix_lengths, TOKENS, MOST)
    suffix_rows = jnp.take(owned_rows, source, axis=0)
    gate_sum = jnp.dot(suffix_rows, gate_weight, preferred_element_type=jnp.float32)
    up_sum = jnp.dot(suffix_rows, up_weight, preferred_element_type=jnp.float32)
    hidden = (jax.nn.silu(gate_sum) * up_sum).astype(jnp.bfloat16)
    return jnp.dot(hidden, down_weight, preferred_element_type=jnp.float32).astype(jnp.bfloat16)
```

```python
import functools

import jax
import jax.numpy as jnp
from jax import lax
from jax.experimental import pallas as pl
from jax.experimental.pallas import tpu as pltpu
from jax.sharding import PartitionSpec as P

TOK_DEV = 8
CHUNK = 512
LAG = 1
WEIGHT_SLOTS = 4
MESH = pl.DeviceIdType.MESH


def source_rows(suffix_lengths, owner_map, prefix_lengths, row_count, slot_size):
    request_ids = jnp.arange(suffix_lengths.shape[0], dtype=jnp.int32)
    longer = prefix_lengths[None, :] > prefix_lengths[:, None]
    earlier = (prefix_lengths[None, :] == prefix_lengths[:, None]) & (
        request_ids[None, :] < request_ids[:, None]
    )
    starts = jnp.sum(jnp.where(longer | earlier, suffix_lengths[None, :], 0), axis=1)
    positions = jnp.arange(row_count, dtype=jnp.int32)
    ends = starts + suffix_lengths
    inside = (positions[:, None] >= starts[None, :]) & (positions[:, None] < ends[None, :])
    offsets = owner_map * slot_size - starts
    shifted = jnp.sum(jnp.where(inside, offsets[None, :], 0), axis=1)
    return positions + shifted


def layer_kernel(
    n, cols, chunks,
    x_ref, gate_ref, up_ref, down_ref, gate_tail, up_tail, down_tail,
    out_ref, *scratch,
):
    k = n.bit_length() - 1
    tokens, width = x_ref.shape[0], gate_tail.shape[1]
    half = tokens // 2
    block = half >> k
    out_width = down_ref.shape[1]
    slots, hidden_slots = 2 * LAG, (k + 1) * LAG
    parts = list(scratch)
    product, hidden, total, gate_w, up_w, down_w, col_out, col_in = parts[:8]
    received = parts[8 : 8 + k]
    outgoing = [None] + parts[8 + k : 7 + 2 * k]
    kept = [None] + parts[7 + 2 * k : 6 + 3 * k]
    send_sem, recv_sem, gather_send, gather_recv, weight_sem, col_send, col_recv = parts[6 + 3 * k :]

    me = lax.axis_index("row")
    my_col = lax.axis_index("col")
    bits = [(me // (1 << b)) % 2 for b in range(k)]
    partners = [me + (1 - 2 * bits[b]) * (1 << b) for b in range(k)]
    orders = [list(range(k)), [0] + list(range(k - 1, 0, -1))]
    places = [sum(bits[b] * (1 << (k - 1 - i)) for i, b in enumerate(order)) for order in orders]

    barrier = pltpu.get_barrier_semaphore()
    for partner in partners:
        pl.semaphore_signal(barrier, inc=1, device_id=(partner, my_col), device_id_type=MESH)
    for step in range(1, cols):
        other = (my_col + step) % cols
        pl.semaphore_signal(barrier, inc=1, device_id=(me, other), device_id_type=MESH)
    pl.semaphore_wait(barrier, k + cols - 1)

    def load(array, tail, buffer, kind, j, by_rows):
        slot = j % WEIGHT_SLOTS
        sem = weight_sem.at[kind, slot]

        @pl.when(j < chunks - 1)
        def _():
            at = pl.ds(pl.multiple_of(j * width, width), width)
            piece = array.at[at, :] if by_rows else array.at[:, at]
            pltpu.make_async_copy(piece, buffer.at[slot], sem).start()

        @pl.when(j == chunks - 1)
        def _():
            pltpu.make_async_copy(tail, buffer.at[slot], sem).start()

    def loaded(tail, buffer, kind, j):
        slot = j % WEIGHT_SLOTS
        pltpu.make_async_copy(tail, buffer.at[slot], weight_sem.at[kind, slot]).wait()

    def load_in(j):
        load(gate_ref, gate_tail, gate_w, 0, j, False)
        load(up_ref, up_tail, up_w, 1, j, False)

    def load_down(j):
        load(down_ref, down_tail, down_w, 2, j, True)

    def exchange(s, h, j):
        slot = j % slots
        b = orders[h][s]
        size = half >> (s + 1)
        if s == 0:
            source = product.at[slot, pl.ds(pl.multiple_of(h * half + (1 - bits[b]) * size, size), size), :]
        else:
            source = outgoing[s].at[slot, h]
        return pltpu.make_async_remote_copy(
            src_ref=source,
            dst_ref=received[s].at[slot, h],
            send_sem=send_sem.at[s, h, slot],
            recv_sem=recv_sem.at[s, h, slot],
            device_id=(partners[b], my_col),
            device_id_type=MESH,
        )

    def gather(i, h, j):
        slot = j % hidden_slots
        b = orders[h][k - 1 - i]
        size = block << i
        at = pl.ds(pl.multiple_of(h * half + places[h] // (1 << i) * size, size), size)
        return pltpu.make_async_remote_copy(
            src_ref=hidden.at[slot, at, :],
            dst_ref=hidden.at[slot, at, :],
            send_sem=gather_send.at[i, h, slot],
            recv_sem=gather_recv.at[i, h, slot],
            device_id=(partners[b], my_col),
            device_id_type=MESH,
        )

    def rows_of(s, h, j, first, size):
        slot = j % slots
        if s == 1:
            at = pl.multiple_of(h * half + bits[orders[h][0]] * (half >> 1) + first, size)
            own = product[slot, pl.ds(at, size), :]
        else:
            own = kept[s - 1][slot, h, pl.ds(first, size), :]
        return own + received[s - 1][slot, h, pl.ds(first, size), :].astype(jnp.float32)

    def halve(s, j):
        size = half >> (s + 1)
        for h in range(2):
            exchange(s - 1, h, j).wait()
            bit = bits[orders[h][s]]
            away = pl.multiple_of((1 - bit) * size, size)
            outgoing[s][j % slots, h] = rows_of(s, h, j, away, size).astype(jnp.bfloat16)
            exchange(s, h, j).start()
        for h in range(2):
            bit = bits[orders[h][s]]
            stay = pl.multiple_of(bit * size, size)
            kept[s][j % slots, h] = rows_of(s, h, j, stay, size)

    def activate(j):
        for h in range(2):
            exchange(k - 1, h, j).wait()
            sums = rows_of(k, h, j, 0, block)
            gate, up = sums[:, :width], sums[:, width:]
            at = pl.multiple_of(h * half + places[h] * block, block)
            value = (gate / (1.0 + jnp.exp(-gate)) * up).astype(jnp.bfloat16)
            hidden[j % hidden_slots, pl.ds(at, block), :] = value
            gather(0, h, j).start()

    def spread(i, j):
        for h in range(2):
            gather(i - 1, h, j).wait_recv()
            gather(i, h, j).start()

    def down(j):
        for h in range(2):
            gather(k - 1, h, j).wait_recv()
        loaded(down_tail, down_w, 2, j)
        total[...] += jnp.dot(
            hidden[j % hidden_slots], down_w[j % WEIGHT_SLOTS], preferred_element_type=jnp.float32
        )
        for i in range(k):
            for h in range(2):
                gather(i, h, j).wait_send()

    def project(j):
        slot = j % slots
        loaded(gate_tail, gate_w, 0, j)
        loaded(up_tail, up_w, 1, j)
        x = x_ref[...]
        product[slot, :, :width] = jnp.dot(
            x, gate_w[j % WEIGHT_SLOTS], preferred_element_type=jnp.float32
        )
        product[slot, :, width:] = jnp.dot(
            x, up_w[j % WEIGHT_SLOTS], preferred_element_type=jnp.float32
        )
        for h in range(2):
            exchange(0, h, j).start()

    steps = [project]
    steps += [functools.partial(halve, s) for s in range(1, k)]
    steps += [activate]
    steps += [functools.partial(spread, i) for i in range(1, k)]
    steps += [down]

    ahead = WEIGHT_SLOTS - 1
    for j in range(min(ahead, chunks)):
        load_in(jnp.int32(j))
        load_down(jnp.int32(j))
    total[...] = jnp.zeros_like(total)
    last = len(steps) - 1

    def round_of(t, carry):
        @pl.when(t + ahead < chunks)
        def _():
            load_in(t + ahead)

        j_down = t - last * LAG + ahead

        @pl.when((j_down >= ahead) & (j_down < chunks))
        def _():
            load_down(j_down)

        for s in range(last, -1, -1):
            j = t - s * LAG

            @pl.when((j >= 0) & (j < chunks))
            def _():
                steps[s](j)

        return carry

    lax.fori_loop(0, chunks + last * LAG, round_of, 0)

    share = tokens // cols
    copies = []
    for step in range(1, cols):
        other = (my_col + step) % cols
        rows = total[pl.ds(pl.multiple_of(other * share, share), share), :]
        col_out[step - 1] = rows.astype(jnp.bfloat16)
        copy = pltpu.make_async_remote_copy(
            src_ref=col_out.at[step - 1],
            dst_ref=col_in.at[step - 1],
            send_sem=col_send.at[step - 1],
            recv_sem=col_recv.at[step - 1],
            device_id=(me, other),
            device_id_type=MESH,
        )
        copy.start()
        copies.append(copy)
    result = total[pl.ds(pl.multiple_of(my_col * share, share), share), :]
    for step, copy in enumerate(copies):
        copy.wait()
        result = result + col_in[step].astype(jnp.float32)
    out_ref[...] = result.astype(jnp.bfloat16)


def layer(x, gate_weight, up_weight, down_weight, n, cols):
    tokens, depth = x.shape
    units = gate_weight.shape[1]
    out_width = down_weight.shape[1]
    width = CHUNK
    chunks = -(-units // width)
    start = (chunks - 1) * width
    short = width - (units - start)
    gate_tail = jnp.pad(gate_weight[:, start:], ((0, 0), (0, short)))
    up_tail = jnp.pad(up_weight[:, start:], ((0, 0), (0, short)))
    down_tail = jnp.pad(down_weight[start:], ((0, short), (0, 0)))
    k = n.bit_length() - 1
    half = tokens // 2
    slots, hidden_slots = 2 * LAG, (k + 1) * LAG
    share = tokens // cols
    bf16, f32 = jnp.bfloat16, jnp.float32
    sizes = [half >> (s + 1) for s in range(k)]
    scratch = [
        pltpu.VMEM((slots, tokens, 2 * width), f32),
        pltpu.VMEM((hidden_slots, tokens, width), bf16),
        pltpu.VMEM((tokens, out_width), f32),
        pltpu.VMEM((WEIGHT_SLOTS, depth, width), bf16),
        pltpu.VMEM((WEIGHT_SLOTS, depth, width), bf16),
        pltpu.VMEM((WEIGHT_SLOTS, width, out_width), bf16),
        pltpu.VMEM((cols - 1, share, out_width), bf16),
        pltpu.VMEM((cols - 1, share, out_width), bf16),
    ]
    scratch += [
        pltpu.VMEM((slots, 2, size, 2 * width), f32 if s == 0 else bf16)
        for s, size in enumerate(sizes)
    ]
    scratch += [pltpu.VMEM((slots, 2, size, 2 * width), bf16) for size in sizes[1:]]
    scratch += [pltpu.VMEM((slots, 2, size, 2 * width), f32) for size in sizes[1:]]
    dma = pltpu.SemaphoreType.DMA
    scratch += [
        dma((k, 2, slots)),
        dma((k, 2, slots)),
        dma((k, 2, hidden_slots)),
        dma((k, 2, hidden_slots)),
        dma((3, WEIGHT_SLOTS)),
        dma((cols - 1,)),
        dma((cols - 1,)),
    ]
    vmem = pl.BlockSpec(memory_space=pltpu.VMEM)
    hbm = pl.BlockSpec(memory_space=pl.ANY)
    return pl.pallas_call(
        functools.partial(layer_kernel, n, cols, chunks),
        out_shape=jax.ShapeDtypeStruct((share, out_width), bf16),
        in_specs=[vmem] + [hbm] * 6,
        out_specs=vmem,
        scratch_shapes=scratch,
        compiler_params=pltpu.CompilerParams(
            collective_id=0, has_side_effects=True, vmem_limit_bytes=56 * 1024 * 1024
        ),
        cost_estimate=pl.CostEstimate(
            flops=6 * tokens * depth * units,
            bytes_accessed=6 * depth * units,
            transcendentals=tokens * units // n,
        ),
    )(x, gate_weight, up_weight, down_weight, gate_tail, up_tail, down_tail)


def on_device(
    owned_rows, suffix_lengths, owner_map, prefix_lengths, gate_weight, up_weight, down_weight
):
    row_count = lax.axis_size("row")
    col_count = lax.axis_size("col")
    slot_size = owned_rows.shape[0]
    total_rows = TOK_DEV * suffix_lengths.shape[0]
    source = source_rows(suffix_lengths, owner_map, prefix_lengths, total_rows, slot_size)
    feature_rows = lax.all_to_all(owned_rows, "row", split_axis=1, concat_axis=0, tiled=True)
    owner_index = source // slot_size
    within = source % slot_size
    gathered_index = (
        owner_index % col_count * row_count + owner_index // col_count
    ) * slot_size + within
    piece = lax.all_gather(feature_rows, "col", axis=0, tiled=True)
    suffix_rows = jnp.take(piece, gathered_index, axis=0, mode="clip")
    return layer(suffix_rows, gate_weight, up_weight, down_weight, row_count, col_count)


def solution(mesh):
    return jax.shard_map(
        on_device,
        mesh=mesh,
        in_specs=(
            P(("row", "col"), None),
            P(),
            P(),
            P(),
            P("row", "col"),
            P("row", "col"),
            P("col", "row"),
        ),
        out_specs=P("col", "row"),
        check_vma=False,
    )
```

```python
import functools

import jax
import jax.numpy as jnp
from jax import lax
from jax.experimental import pallas as pl
from jax.experimental.pallas import tpu as pltpu
from jax.sharding import PartitionSpec as P

TOK_DEV = 8
CHUNK = 256
LAG = 2
WEIGHT_SLOTS = 6
PIECE = 128
MESH = pl.DeviceIdType.MESH


def source_rows(suffix_lengths, owner_map, prefix_lengths, row_count, slot_size):
    request_ids = jnp.arange(suffix_lengths.shape[0], dtype=jnp.int32)
    longer = prefix_lengths[None, :] > prefix_lengths[:, None]
    earlier = (prefix_lengths[None, :] == prefix_lengths[:, None]) & (
        request_ids[None, :] < request_ids[:, None]
    )
    starts = jnp.sum(jnp.where(longer | earlier, suffix_lengths[None, :], 0), axis=1)
    positions = jnp.arange(row_count, dtype=jnp.int32)
    ends = starts + suffix_lengths
    inside = (positions[:, None] >= starts[None, :]) & (positions[:, None] < ends[None, :])
    offsets = owner_map * slot_size - starts
    shifted = jnp.sum(jnp.where(inside, offsets[None, :], 0), axis=1)
    return positions + shifted


def layer_kernel(
    n, cols, chunks,
    blocks_ref, place_ref, gate_ref, up_ref, down_ref,
    out_ref, *scratch,
):
    k = n.bit_length() - 1
    tokens, width = place_ref.shape[0], CHUNK
    rest = gate_ref.shape[0] - (chunks - 1) * width
    half = tokens // 2
    block = half >> k
    out_width = down_ref.shape[1]
    slots, hidden_slots = 2 * LAG, (k + 1) * LAG
    parts = list(scratch)
    product, hidden, total, gate_w, up_w, down_w, col_out, col_in = parts[:8]
    received = parts[8 : 8 + k]
    outgoing = [None] + parts[8 + k : 7 + 2 * k]
    kept = [None] + parts[7 + 2 * k : 6 + 3 * k]
    send_sem, recv_sem, gather_send, gather_recv, weight_sem, col_send, col_recv = parts[
        6 + 3 * k : 13 + 3 * k
    ]
    x_ref, plane, own, line_out, line_in, block_send, block_recv, line_send, line_recv = parts[
        13 + 3 * k :
    ]

    me = lax.axis_index("row")
    my_col = lax.axis_index("col")
    bits = [(me // (1 << b)) % 2 for b in range(k)]
    partners = [me + (1 - 2 * bits[b]) * (1 << b) for b in range(k)]
    orders = [list(range(k)), [0] + list(range(k - 1, 0, -1))]
    places = [sum(bits[b] * (1 << (k - 1 - i)) for i, b in enumerate(order)) for order in orders]

    barrier = pltpu.get_barrier_semaphore()
    for step in range(1, n):
        other = (me + step) % n
        pl.semaphore_signal(barrier, inc=1, device_id=(other, my_col), device_id_type=MESH)
    for step in range(1, cols):
        other = (my_col + step) % cols
        pl.semaphore_signal(barrier, inc=1, device_id=(me, other), device_id_type=MESH)
    pl.semaphore_wait(barrier, n - 1 + cols - 1)

    def weight_copy(kind, j, rows):
        array, buffer = ((gate_ref, gate_w), (up_ref, up_w), (down_ref, down_w))[kind]
        slot = j % WEIGHT_SLOTS
        return pltpu.make_async_copy(
            array.at[pl.ds(pl.multiple_of(j * width, width), rows), :],
            buffer.at[slot, pl.ds(0, rows), :],
            weight_sem.at[kind, slot],
        )

    def load(kind, j):
        @pl.when(j < chunks - 1)
        def _():
            weight_copy(kind, j, width).start()

        @pl.when(j == chunks - 1)
        def _():
            if rest < width:
                buffer = (gate_w, up_w, down_w)[kind]
                shape = (width - rest, buffer.shape[2])
                buffer[j % WEIGHT_SLOTS, rest:, :] = jnp.zeros(shape, jnp.bfloat16)
            weight_copy(kind, chunks - 1, rest).start()

    def loaded(kind, j):
        @pl.when(j < chunks - 1)
        def _():
            weight_copy(kind, j, width).wait()

        @pl.when(j == chunks - 1)
        def _():
            weight_copy(kind, chunks - 1, rest).wait()

    def load_in(j):
        load(0, j)
        load(1, j)

    def load_down(j):
        load(2, j)

    def exchange(s, h, j):
        slot = j % slots
        b = orders[h][s]
        size = half >> (s + 1)
        if s == 0:
            source = product.at[slot, pl.ds(pl.multiple_of(h * half + (1 - bits[b]) * size, size), size), :]
        else:
            source = outgoing[s].at[slot, h]
        return pltpu.make_async_remote_copy(
            src_ref=source,
            dst_ref=received[s].at[slot, h],
            send_sem=send_sem.at[s, h, slot],
            recv_sem=recv_sem.at[s, h, slot],
            device_id=(partners[b], my_col),
            device_id_type=MESH,
        )

    def gather(i, h, j):
        slot = j % hidden_slots
        b = orders[h][k - 1 - i]
        size = block << i
        at = pl.ds(pl.multiple_of(h * half + places[h] // (1 << i) * size, size), size)
        return pltpu.make_async_remote_copy(
            src_ref=hidden.at[slot, at, :],
            dst_ref=hidden.at[slot, at, :],
            send_sem=gather_send.at[i, h, slot],
            recv_sem=gather_recv.at[i, h, slot],
            device_id=(partners[b], my_col),
            device_id_type=MESH,
        )

    def rows_of(s, h, j, first, size):
        slot = j % slots
        if s == 1:
            at = pl.multiple_of(h * half + bits[orders[h][0]] * (half >> 1) + first, size)
            own = product[slot, pl.ds(at, size), :]
        else:
            own = kept[s - 1][slot, h, pl.ds(first, size), :]
        return own + received[s - 1][slot, h, pl.ds(first, size), :].astype(jnp.float32)

    def halve(s, j):
        size = half >> (s + 1)
        for h in range(2):
            exchange(s - 1, h, j).wait()
            bit = bits[orders[h][s]]
            away = pl.multiple_of((1 - bit) * size, size)
            outgoing[s][j % slots, h] = rows_of(s, h, j, away, size).astype(jnp.bfloat16)
            exchange(s, h, j).start()
        for h in range(2):
            bit = bits[orders[h][s]]
            stay = pl.multiple_of(bit * size, size)
            kept[s][j % slots, h] = rows_of(s, h, j, stay, size)

    def activate(j):
        for h in range(2):
            exchange(k - 1, h, j).wait()
            sums = rows_of(k, h, j, 0, block)
            gate, up = sums[:, :width], sums[:, width:]
            at = pl.multiple_of(h * half + places[h] * block, block)
            value = (gate / (1.0 + jnp.exp(-gate)) * up).astype(jnp.bfloat16)
            hidden[j % hidden_slots, pl.ds(at, block), :] = value
            gather(0, h, j).start()

    def spread(i, j):
        for h in range(2):
            gather(i - 1, h, j).wait_recv()
            gather(i, h, j).start()

    def down(j):
        for h in range(2):
            gather(k - 1, h, j).wait_recv()
        loaded(2, j)
        total[...] += jnp.dot(
            hidden[j % hidden_slots], down_w[j % WEIGHT_SLOTS], preferred_element_type=jnp.float32
        )
        for i in range(k):
            for h in range(2):
                gather(i, h, j).wait_send()

    def project(j):
        slot = j % slots
        loaded(0, j)
        loaded(1, j)
        x = x_ref[...]
        features = (((1,), (1,)), ((), ()))
        product[slot, :, :width] = lax.dot_general(
            x, gate_w[j % WEIGHT_SLOTS], features, preferred_element_type=jnp.float32
        )
        product[slot, :, width:] = lax.dot_general(
            x, up_w[j % WEIGHT_SLOTS], features, preferred_element_type=jnp.float32
        )
        for h in range(2):
            exchange(0, h, j).start()

    pieces = own.shape[0]
    deep = blocks_ref.shape[1]

    def block_copy(step):
        other = (me + step) % n
        return pltpu.make_async_remote_copy(
            src_ref=blocks_ref.at[other],
            dst_ref=plane.at[pl.ds(pl.multiple_of(me * deep, deep), deep), :],
            send_sem=block_send.at[step - 1],
            recv_sem=block_recv.at[step - 1],
            device_id=(other, my_col),
            device_id_type=MESH,
        )

    def line_copy(way, f):
        return pltpu.make_async_remote_copy(
            src_ref=line_out.at[way, f],
            dst_ref=line_in.at[way, f],
            send_sem=line_send.at[way, f],
            recv_sem=line_recv.at[way, f],
            device_id=(me, (my_col + (1 if way == 0 else cols - 1)) % cols),
            device_id_type=MESH,
        )

    def gather_rows():
        copies = [block_copy(step) for step in range(1, n)]
        for copy in copies:
            copy.start()
        plane[pl.ds(pl.multiple_of(me * deep, deep), deep), :] = blocks_ref[me]
        column = lax.broadcasted_iota(jnp.int32, (tokens, n * deep), 1)
        behind = [my_col, cols - 1 - my_col]
        for way in range(2):
            @pl.when(behind[way] == 0)
            def _():
                line_in[way] = jnp.zeros(line_in.shape[1:], jnp.bfloat16)

        for copy in copies:
            copy.wait()
        for part in range(2):
            pick = (column == place_ref[...] + part * (deep // 2)).astype(jnp.bfloat16)
            rows = jnp.dot(pick, plane[...], preferred_element_type=jnp.float32)
            rows = rows.astype(jnp.bfloat16)
            for f in range(pieces // 2):
                own[part * (pieces // 2) + f] = rows[:, f * PIECE : (f + 1) * PIECE]

        def pass_on(u, carry):
            for way in range(2):
                f = u - 2 * behind[way]

                @pl.when((f >= 0) & (f < pieces))
                def _():
                    @pl.when(behind[way] > 0)
                    def _():
                        line_copy(way, f).wait_recv()

                    @pl.when(behind[way] < cols - 1)
                    def _():
                        line_out[way, f] = own[f] + line_in[way, f]
                        line_copy(way, f).start()

            return carry

        lax.fori_loop(0, pieces + 2 * (cols - 1), pass_on, 0)
        for f in range(pieces):
            at = slice(f * PIECE, (f + 1) * PIECE)
            x_ref[:, at] = own[f] + line_in[0, f] + line_in[1, f]

    def end_gather():
        for way in range(2):
            @pl.when([my_col, cols - 1 - my_col][way] < cols - 1)
            def _():
                for f in range(pieces):
                    line_copy(way, f).wait_send()

    steps = [project]
    steps += [functools.partial(halve, s) for s in range(1, k)]
    steps += [activate]
    steps += [functools.partial(spread, i) for i in range(1, k)]
    steps += [down]

    ahead = WEIGHT_SLOTS - 1
    for j in range(min(ahead, chunks)):
        load_in(jnp.int32(j))
        load_down(jnp.int32(j))
    total[...] = jnp.zeros_like(total)
    gather_rows()
    last = len(steps) - 1

    def round_of(t, carry):
        @pl.when(t + ahead < chunks)
        def _():
            load_in(t + ahead)

        j_down = t - last * LAG + ahead

        @pl.when((j_down >= ahead) & (j_down < chunks))
        def _():
            load_down(j_down)

        for s in range(last, -1, -1):
            j = t - s * LAG

            @pl.when((j >= 0) & (j < chunks))
            def _():
                steps[s](j)

        return carry

    lax.fori_loop(0, chunks + last * LAG, round_of, 0)

    end_gather()
    share = tokens // cols
    copies = []
    for step in range(1, cols):
        other = (my_col + step) % cols
        rows = total[pl.ds(pl.multiple_of(other * share, share), share), :]
        col_out[step - 1] = rows.astype(jnp.bfloat16)
        copy = pltpu.make_async_remote_copy(
            src_ref=col_out.at[step - 1],
            dst_ref=col_in.at[step - 1],
            send_sem=col_send.at[step - 1],
            recv_sem=col_recv.at[step - 1],
            device_id=(me, other),
            device_id_type=MESH,
        )
        copy.start()
        copies.append(copy)
    result = total[pl.ds(pl.multiple_of(my_col * share, share), share), :]
    for step, copy in enumerate(copies):
        copy.wait()
        result = result + col_in[step].astype(jnp.float32)
    out_ref[...] = result.astype(jnp.bfloat16)


def layer(blocks, place, gate_weight, up_weight, down_weight, n, cols):
    tokens = place.shape[0]
    units, depth = gate_weight.shape
    out_width = down_weight.shape[1]
    width = CHUNK
    chunks = -(-units // width)
    k = n.bit_length() - 1
    half = tokens // 2
    slots, hidden_slots = 2 * LAG, (k + 1) * LAG
    share = tokens // cols
    bf16, f32 = jnp.bfloat16, jnp.float32
    sizes = [half >> (s + 1) for s in range(k)]
    scratch = [
        pltpu.VMEM((slots, tokens, 2 * width), f32),
        pltpu.VMEM((hidden_slots, tokens, width), bf16),
        pltpu.VMEM((tokens, out_width), f32),
        pltpu.VMEM((WEIGHT_SLOTS, width, depth), bf16),
        pltpu.VMEM((WEIGHT_SLOTS, width, depth), bf16),
        pltpu.VMEM((WEIGHT_SLOTS, width, out_width), bf16),
        pltpu.VMEM((cols - 1, share, out_width), bf16),
        pltpu.VMEM((cols - 1, share, out_width), bf16),
    ]
    scratch += [
        pltpu.VMEM((slots, 2, size, 2 * width), f32 if s == 0 else bf16)
        for s, size in enumerate(sizes)
    ]
    scratch += [pltpu.VMEM((slots, 2, size, 2 * width), bf16) for size in sizes[1:]]
    scratch += [pltpu.VMEM((slots, 2, size, 2 * width), f32) for size in sizes[1:]]
    dma = pltpu.SemaphoreType.DMA
    scratch += [
        dma((k, 2, slots)),
        dma((k, 2, slots)),
        dma((k, 2, hidden_slots)),
        dma((k, 2, hidden_slots)),
        dma((3, WEIGHT_SLOTS)),
        dma((cols - 1,)),
        dma((cols - 1,)),
    ]
    pieces = depth // PIECE
    scratch += [
        pltpu.VMEM((tokens, depth), bf16),
        pltpu.VMEM((n * blocks.shape[1], depth // 2), bf16),
        pltpu.VMEM((pieces, tokens, PIECE), bf16),
        pltpu.VMEM((2, pieces, tokens, PIECE), bf16),
        pltpu.VMEM((2, pieces, tokens, PIECE), bf16),
        dma((n - 1,)),
        dma((n - 1,)),
        dma((2, pieces)),
        dma((2, pieces)),
    ]
    vmem = pl.BlockSpec(memory_space=pltpu.VMEM)
    hbm = pl.BlockSpec(memory_space=pl.ANY)
    return pl.pallas_call(
        functools.partial(layer_kernel, n, cols, chunks),
        out_shape=jax.ShapeDtypeStruct((share, out_width), bf16),
        in_specs=[vmem] * 2 + [hbm] * 3,
        out_specs=vmem,
        scratch_shapes=scratch,
        compiler_params=pltpu.CompilerParams(
            collective_id=0, has_side_effects=True, vmem_limit_bytes=56 * 1024 * 1024
        ),
        cost_estimate=pl.CostEstimate(
            flops=6 * tokens * depth * units,
            bytes_accessed=6 * depth * units,
            transcendentals=tokens * units // n,
        ),
    )(blocks, place, gate_weight, up_weight, down_weight)


def on_device(
    owned_rows, suffix_lengths, owner_map, prefix_lengths, gate_weight, up_weight, down_weight
):
    row_count = lax.axis_size("row")
    col_count = lax.axis_size("col")
    slot_size = owned_rows.shape[0]
    total_rows = TOK_DEV * suffix_lengths.shape[0]
    source = source_rows(suffix_lengths, owner_map, prefix_lengths, total_rows, slot_size)
    owner = source // slot_size
    deep = 2 * slot_size
    place = jnp.where(
        owner % col_count == lax.axis_index("col"),
        owner // col_count * deep + source % slot_size,
        -2 * deep,
    )
    blocks = owned_rows.reshape(slot_size, row_count, 2, -1).transpose(1, 2, 0, 3)
    blocks = blocks.reshape(row_count, deep, -1)
    return layer(
        blocks, place[:, None], gate_weight.T, up_weight.T, down_weight, row_count, col_count
    )


def solution(mesh):
    return jax.shard_map(
        on_device,
        mesh=mesh,
        in_specs=(
            P(("row", "col"), None),
            P(),
            P(),
            P(),
            P("row", "col"),
            P("row", "col"),
            P("col", "row"),
        ),
        out_specs=P("col", "row"),
        check_vma=False,
    )
```

```python
import functools

import jax
import jax.numpy as jnp
from jax import lax
from jax.experimental import pallas as pl
from jax.experimental.pallas import tpu as pltpu
from jax.sharding import PartitionSpec as P

TOK_DEV = 8
CHUNK = 512
BATCHES = 2
LAG = 2
WEIGHT_SLOTS = 4
PIECE = 128
MESH = pl.DeviceIdType.MESH


def layer_kernel(
    n, cols, chunks, batches,
    lengths_ref, owner_ref, prefix_ref, blocks_ref, gate_ref, up_ref, down_ref, out_ref,
    product, hidden, total, gate_w, up_w, down_w, col_out, col_in,
    x_ref, plane, own, line_out, line_in,
    send_sem, recv_sem, gather_send, gather_recv, weight_sem, col_send, col_recv,
    block_send, block_recv, line_send, line_recv, *stages,
):
    k = n.bit_length() - 1
    width, tokens = CHUNK, x_ref.shape[1]
    every = batches * chunks
    rest = gate_ref.shape[0] - (chunks - 1) * width
    block = tokens >> k
    part = tokens // cols
    slots, hidden_slots = 2 * LAG, (k + 1) * LAG
    received = stages[:k]
    outgoing = (None,) + stages[k : 2 * k - 1]
    kept = (None,) + stages[2 * k - 1 :]

    me = lax.axis_index("row")
    my_col = lax.axis_index("col")
    bits = [(me // (1 << b)) % 2 for b in range(k)]
    partners = [me + (1 - 2 * bits[b]) * (1 << b) for b in range(k)]
    orders = [list(range(k)), [0] + list(range(k - 1, 0, -1))]
    places = [sum(bits[b] * (1 << (k - 1 - i)) for i, b in enumerate(order)) for order in orders]

    def by_turn(values, j):
        return values[0] + (j % 2) * (values[1] - values[0])

    def bit_of(s, j):
        return by_turn([bits[order[s]] for order in orders], j)

    def partner_of(s, j):
        return by_turn([partners[order[s]] for order in orders], j)

    barrier = pltpu.get_barrier_semaphore()
    for step in range(1, n):
        other = (me + step) % n
        pl.semaphore_signal(barrier, inc=1, device_id=(other, my_col), device_id_type=MESH)
    for step in range(1, cols):
        other = (my_col + step) % cols
        pl.semaphore_signal(barrier, inc=1, device_id=(me, other), device_id_type=MESH)
    pl.semaphore_wait(barrier, n - 1 + cols - 1)

    def weight_copy(kind, j, rows):
        array, buffer = ((gate_ref, gate_w), (up_ref, up_w), (down_ref, down_w))[kind]
        slot = j % WEIGHT_SLOTS
        first = pl.multiple_of(j % chunks * width, width)
        return pltpu.make_async_copy(
            array.at[pl.ds(first, rows), :],
            buffer.at[slot, pl.ds(0, rows), :],
            weight_sem.at[kind, slot],
        )

    def load(kind, j):
        @pl.when(j % chunks < chunks - 1)
        def _():
            weight_copy(kind, j, width).start()

        @pl.when(j % chunks == chunks - 1)
        def _():
            if rest < width:
                buffer = (gate_w, up_w, down_w)[kind]
                shape = (width - rest, buffer.shape[2])
                buffer[j % WEIGHT_SLOTS, rest:, :] = jnp.zeros(shape, jnp.bfloat16)
            weight_copy(kind, j, rest).start()

    def loaded(kind, j):
        @pl.when(j % chunks < chunks - 1)
        def _():
            weight_copy(kind, j, width).wait()

        @pl.when(j % chunks == chunks - 1)
        def _():
            weight_copy(kind, j, rest).wait()

    def exchange(s, j):
        slot = j % slots
        size = tokens >> (s + 1)
        if s == 0:
            at = pl.multiple_of((1 - bits[0]) * size, size)
            source = product.at[slot, pl.ds(at, size), :]
        else:
            source = outgoing[s].at[slot]
        return pltpu.make_async_remote_copy(
            src_ref=source,
            dst_ref=received[s].at[slot],
            send_sem=send_sem.at[s, slot],
            recv_sem=recv_sem.at[s, slot],
            device_id=(partner_of(s, j), my_col),
            device_id_type=MESH,
        )

    def gather(i, j):
        slot = j % hidden_slots
        size = block << i
        at = pl.ds(pl.multiple_of(by_turn(places, j) // (1 << i) * size, size), size)
        return pltpu.make_async_remote_copy(
            src_ref=hidden.at[slot, at, :],
            dst_ref=hidden.at[slot, at, :],
            send_sem=gather_send.at[i, slot],
            recv_sem=gather_recv.at[i, slot],
            device_id=(partner_of(k - 1 - i, j), my_col),
            device_id_type=MESH,
        )

    def rows_of(s, j, first, size):
        slot = j % slots
        if s == 1:
            at = pl.multiple_of(bits[0] * (tokens >> 1) + first, size)
            mine = product[slot, pl.ds(at, size), :]
        else:
            mine = kept[s - 1][slot, pl.ds(first, size), :]
        return mine + received[s - 1][slot, pl.ds(first, size), :].astype(jnp.float32)

    def halve(s, j):
        size = tokens >> (s + 1)
        slot = j % slots
        bit = bit_of(s, j)
        away = pl.multiple_of((1 - bit) * size, size)
        stay = pl.multiple_of(bit * size, size)
        exchange(s - 1, j).wait()
        outgoing[s][slot] = rows_of(s, j, away, size).astype(jnp.bfloat16)
        exchange(s, j).start()
        kept[s][slot] = rows_of(s, j, stay, size)

    def activate(j):
        exchange(k - 1, j).wait()
        sums = rows_of(k, j, 0, block)
        gate, up = sums[:, :width], sums[:, width:]
        at = pl.multiple_of(by_turn(places, j) * block, block)
        value = (gate / (1.0 + jnp.exp(-gate)) * up).astype(jnp.bfloat16)
        hidden[j % hidden_slots, pl.ds(at, block), :] = value
        gather(0, j).start()

    def spread(i, j):
        gather(i - 1, j).wait_recv()
        gather(i, j).start()

    def down(j):
        gather(k - 1, j).wait_recv()
        loaded(2, j)
        total[j // chunks] += jnp.dot(
            hidden[j % hidden_slots], down_w[j % WEIGHT_SLOTS], preferred_element_type=jnp.float32
        )
        for i in range(k):
            gather(i, j).wait_send()

    def project(j):
        slot = j % slots
        loaded(0, j)
        loaded(1, j)
        x = x_ref[j // chunks]
        features = (((1,), (1,)), ((), ()))
        product[slot, :, :width] = lax.dot_general(
            x, gate_w[j % WEIGHT_SLOTS], features, preferred_element_type=jnp.float32
        )
        product[slot, :, width:] = lax.dot_general(
            x, up_w[j % WEIGHT_SLOTS], features, preferred_element_type=jnp.float32
        )
        exchange(0, j).start()

    steps = [project]
    steps += [functools.partial(halve, s) for s in range(1, k)]
    steps += [activate]
    steps += [functools.partial(spread, i) for i in range(1, k)]
    steps += [down]
    last = len(steps) - 1

    pieces = own.shape[1]
    deep = blocks_ref.shape[1]
    behind = [my_col, cols - 1 - my_col]
    line_steps = pieces + 2 * (cols - 1)

    def block_copy(step):
        other = (me + step) % n
        return pltpu.make_async_remote_copy(
            src_ref=blocks_ref.at[other],
            dst_ref=plane.at[pl.ds(pl.multiple_of(me * deep, deep), deep), :],
            send_sem=block_send.at[step - 1],
            recv_sem=block_recv.at[step - 1],
            device_id=(other, my_col),
            device_id_type=MESH,
        )

    def line_copy(batch, way, f):
        return pltpu.make_async_remote_copy(
            src_ref=line_out.at[batch, way, f],
            dst_ref=line_in.at[batch, way, f],
            send_sem=line_send.at[batch, way, f],
            recv_sem=line_recv.at[batch, way, f],
            device_id=(me, (my_col + (1 if way == 0 else cols - 1)) % cols),
            device_id_type=MESH,
        )

    def place_rows():
        count = lengths_ref.shape[1]
        f32 = jnp.float32
        lengths = lengths_ref[...].astype(f32)
        prefix = prefix_ref[...].astype(f32)
        owner = owner_ref[...]
        down_id = lax.broadcasted_iota(jnp.int32, (count, count), 0)
        over_id = lax.broadcasted_iota(jnp.int32, (count, count), 1)
        same = down_id == over_id
        lengths_down = jnp.sum(jnp.where(same, lengths, 0.0), axis=1, keepdims=True)
        prefix_down = jnp.sum(jnp.where(same, prefix, 0.0), axis=1, keepdims=True)
        before = (prefix_down > prefix) | ((prefix_down == prefix) & (down_id < over_id))
        starts = jnp.sum(jnp.where(before, lengths_down, 0.0), axis=0, keepdims=True)
        first = (owner // cols * deep).astype(f32) - starts
        first = jnp.where(owner % cols == my_col, first, -1e6)
        row = lax.broadcasted_iota(jnp.int32, (batches * tokens, 1), 0)
        batch, at = row // tokens, row % tokens
        token = ((at // part * batches + batch) * part + at % part).astype(f32)
        inside = (token >= starts) & (token < starts + lengths)
        return token + jnp.sum(jnp.where(inside, first, 0.0), axis=1, keepdims=True)

    def pick(batch, place):
        column = lax.broadcasted_iota(jnp.int32, (tokens, n * deep), 1).astype(jnp.float32)
        for side in range(2):
            chosen = (column == place + float(side * (deep // 2))).astype(jnp.bfloat16)
            rows = jnp.dot(chosen, plane[...], preferred_element_type=jnp.float32)
            rows = rows.astype(jnp.bfloat16)
            for f in range(pieces // 2):
                own[batch, side * (pieces // 2) + f] = rows[:, f * PIECE : (f + 1) * PIECE]

    def pass_on(batch, u):
        for way in range(2):
            f = u - 2 * behind[way]

            @pl.when((f >= 0) & (f < pieces))
            def _():
                @pl.when(behind[way] > 0)
                def _():
                    line_copy(batch, way, f).wait_recv()

                @pl.when(behind[way] < cols - 1)
                def _():
                    line_out[batch, way, f] = own[batch, f] + line_in[batch, way, f]
                    line_copy(batch, way, f).start()

    def join(batch):
        for f in range(pieces):
            at = slice(f * PIECE, (f + 1) * PIECE)
            x_ref[batch, :, at] = own[batch, f] + line_in[batch, 0, f] + line_in[batch, 1, f]

    def col_copy(batch, step):
        return pltpu.make_async_remote_copy(
            src_ref=col_out.at[batch, step - 1],
            dst_ref=col_in.at[batch, step - 1],
            send_sem=col_send.at[batch, step - 1],
            recv_sem=col_recv.at[batch, step - 1],
            device_id=(me, (my_col + step) % cols),
            device_id_type=MESH,
        )

    def send_cols(batch):
        for step in range(1, cols):
            other = (my_col + step) % cols
            rows = total[batch, pl.ds(pl.multiple_of(other * part, part), part), :]
            col_out[batch, step - 1] = rows.astype(jnp.bfloat16)
            col_copy(batch, step).start()

    for step in range(1, n):
        block_copy(step).start()
    ahead = WEIGHT_SLOTS - 1
    for j in range(min(ahead, every)):
        for kind in range(3):
            load(kind, jnp.int32(j))
    plane[pl.ds(pl.multiple_of(me * deep, deep), deep), :] = blocks_ref[me]
    total[...] = jnp.zeros_like(total)
    for way in range(2):
        @pl.when(behind[way] == 0)
        def _():
            for batch in range(batches):
                line_in[batch, way] = jnp.zeros(line_in.shape[2:], jnp.bfloat16)

    place = place_rows()
    for step in range(1, n):
        block_copy(step).wait()
    for batch in range(batches):
        pick(batch, place[batch * tokens : (batch + 1) * tokens])

    def first_line(u, carry):
        pass_on(0, u)
        return carry

    lax.fori_loop(0, line_steps, first_line, 0)
    join(0)
    per_round = -(-line_steps // chunks)

    def round_of(t, carry):
        @pl.when(t + ahead < every)
        def _():
            load(0, t + ahead)
            load(1, t + ahead)

        j_down = t - last * LAG + ahead

        @pl.when((j_down >= ahead) & (j_down < every))
        def _():
            load(2, j_down)

        for batch in range(1, batches):
            @pl.when(t == batch * chunks)
            def _():
                join(batch)

        for s in range(last, -1, -1):
            j = t - s * LAG

            @pl.when((j >= 0) & (j < every))
            def _():
                steps[s](j)

        for batch in range(1, batches):
            for q in range(per_round):
                pass_on(batch, (t - (batch - 1) * chunks) * per_round + q)

        for batch in range(batches):
            @pl.when(t == (batch + 1) * chunks - 1 + last * LAG)
            def _():
                send_cols(batch)

        return carry

    lax.fori_loop(0, every + last * LAG, round_of, 0)

    for batch in range(batches):
        for way in range(2):
            @pl.when(behind[way] < cols - 1)
            def _():
                for f in range(pieces):
                    line_copy(batch, way, f).wait_send()

    for batch in range(batches):
        result = total[batch, pl.ds(pl.multiple_of(my_col * part, part), part), :]
        for step in range(1, cols):
            col_copy(batch, step).wait()
            result = result + col_in[batch, step - 1].astype(jnp.float32)
        out_ref[batch * part : (batch + 1) * part, :] = result.astype(jnp.bfloat16)


def on_device(
    owned_rows, suffix_lengths, owner_map, prefix_lengths, gate_weight, up_weight, down_weight
):
    n, cols = lax.axis_size("row"), lax.axis_size("col")
    slot_size = owned_rows.shape[0]
    all_tokens = TOK_DEV * suffix_lengths.shape[0]
    depth, units = gate_weight.shape
    out_width = down_weight.shape[1]
    deep = 2 * slot_size
    blocks = owned_rows.reshape(slot_size, n, 2, depth // 2).transpose(1, 2, 0, 3)
    blocks = blocks.reshape(n, deep, depth // 2)

    width, batches = CHUNK, BATCHES
    tokens = all_tokens // batches
    chunks = -(-units // width)
    k = n.bit_length() - 1
    slots, hidden_slots = 2 * LAG, (k + 1) * LAG
    part = tokens // cols
    pieces = depth // PIECE
    bf16, f32 = jnp.bfloat16, jnp.float32
    dma = pltpu.SemaphoreType.DMA
    scratch = [
        pltpu.VMEM((slots, tokens, 2 * width), f32),
        pltpu.VMEM((hidden_slots, tokens, width), bf16),
        pltpu.VMEM((batches, tokens, out_width), f32),
        pltpu.VMEM((WEIGHT_SLOTS, width, depth), bf16),
        pltpu.VMEM((WEIGHT_SLOTS, width, depth), bf16),
        pltpu.VMEM((WEIGHT_SLOTS, width, out_width), bf16),
        pltpu.VMEM((batches, cols - 1, part, out_width), bf16),
        pltpu.VMEM((batches, cols - 1, part, out_width), bf16),
        pltpu.VMEM((batches, tokens, depth), bf16),
        pltpu.VMEM((n * deep, depth // 2), bf16),
        pltpu.VMEM((batches, pieces, tokens, PIECE), bf16),
        pltpu.VMEM((batches, 2, pieces, tokens, PIECE), bf16),
        pltpu.VMEM((batches, 2, pieces, tokens, PIECE), bf16),
        dma((k, slots)),
        dma((k, slots)),
        dma((k, hidden_slots)),
        dma((k, hidden_slots)),
        dma((3, WEIGHT_SLOTS)),
        dma((batches, cols - 1)),
        dma((batches, cols - 1)),
        dma((n - 1,)),
        dma((n - 1,)),
        dma((batches, 2, pieces)),
        dma((batches, 2, pieces)),
    ]
    sizes = [tokens >> (s + 1) for s in range(k)]
    scratch += [
        pltpu.VMEM((slots, size, 2 * width), f32 if s == 0 else bf16)
        for s, size in enumerate(sizes)
    ]
    scratch += [pltpu.VMEM((slots, size, 2 * width), bf16) for size in sizes[1:]]
    scratch += [pltpu.VMEM((slots, size, 2 * width), f32) for size in sizes[1:]]
    vmem = pl.BlockSpec(memory_space=pltpu.VMEM)
    hbm = pl.BlockSpec(memory_space=pl.ANY)
    return pl.pallas_call(
        functools.partial(layer_kernel, n, cols, chunks, batches),
        out_shape=jax.ShapeDtypeStruct((batches * part, out_width), bf16),
        in_specs=[vmem] * 4 + [hbm] * 3,
        out_specs=vmem,
        scratch_shapes=scratch,
        compiler_params=pltpu.CompilerParams(
            collective_id=0, has_side_effects=True, vmem_limit_bytes=56 * 1024 * 1024
        ),
        cost_estimate=pl.CostEstimate(
            flops=6 * all_tokens * depth * units,
            bytes_accessed=6 * depth * units * batches,
            transcendentals=all_tokens * units // n,
        ),
    )(
        suffix_lengths[None],
        owner_map[None],
        prefix_lengths[None],
        blocks,
        gate_weight.T,
        up_weight.T,
        down_weight,
    )


def solution(mesh):
    return jax.shard_map(
        on_device,
        mesh=mesh,
        in_specs=(
            P(("row", "col"), None),
            P(),
            P(),
            P(),
            P("row", "col"),
            P("row", "col"),
            P("col", "row"),
        ),
        out_specs=P("col", "row"),
        check_vma=False,
    )
```

```python
import functools

import jax
import jax.numpy as jnp
from jax import lax
from jax.experimental import pallas as pl
from jax.experimental.pallas import tpu as pltpu
from jax.sharding import PartitionSpec as P

TOK_DEV = 8
CHUNK = 512
BATCHES = 2
LAG = 2
WEIGHT_SLOTS = 4
PIECE = 128
MESH = pl.DeviceIdType.MESH


def layer_kernel(
    n, cols, chunks, batches,
    lengths_ref, owner_ref, prefix_ref, blocks_ref, gate_ref, up_ref, down_ref, out_ref,
    product, hidden, total, gate_w, up_w, down_w, col_out, col_in,
    x_ref, plane, own, line_out, line_in,
    send_sem, recv_sem, gather_send, gather_recv, weight_sem, col_send, col_recv,
    block_send, block_recv, line_send, line_recv, *stages,
):
    k = n.bit_length() - 1
    width, tokens = CHUNK, x_ref.shape[2]
    every = batches * chunks
    rest = gate_ref.shape[0] - (chunks - 1) * width
    block = width >> k
    part = tokens // cols
    slots, hidden_slots = 2 * LAG, (k + 1) * LAG
    received = stages[:k]
    outgoing = (None,) + stages[k : 2 * k - 1]
    kept = (None,) + stages[2 * k - 1 :]

    me = lax.axis_index("row")
    my_col = lax.axis_index("col")
    bits = [(me // (1 << b)) % 2 for b in range(k)]
    partners = [me + (1 - 2 * bits[b]) * (1 << b) for b in range(k)]
    orders = [list(range(k)), [0] + list(range(k - 1, 0, -1))]
    places = [sum(bits[b] * (1 << (k - 1 - i)) for i, b in enumerate(order)) for order in orders]

    def by_turn(values, j):
        return values[0] + (j % 2) * (values[1] - values[0])

    def bit_of(s, j):
        return by_turn([bits[order[s]] for order in orders], j)

    def partner_of(s, j):
        return by_turn([partners[order[s]] for order in orders], j)

    barrier = pltpu.get_barrier_semaphore()
    for step in range(1, n):
        other = (me + step) % n
        pl.semaphore_signal(barrier, inc=1, device_id=(other, my_col), device_id_type=MESH)
    for step in range(1, cols):
        other = (my_col + step) % cols
        pl.semaphore_signal(barrier, inc=1, device_id=(me, other), device_id_type=MESH)
    pl.semaphore_wait(barrier, n - 1 + cols - 1)

    def weight_copy(kind, j, rows):
        array, buffer = ((gate_ref, gate_w), (up_ref, up_w), (down_ref, down_w))[kind]
        slot = j % WEIGHT_SLOTS
        first = pl.multiple_of(j % chunks * width, width)
        return pltpu.make_async_copy(
            array.at[pl.ds(first, rows), :],
            buffer.at[slot, pl.ds(0, rows), :],
            weight_sem.at[kind, slot],
        )

    def load(kind, j):
        @pl.when(j % chunks < chunks - 1)
        def _():
            weight_copy(kind, j, width).start()

        @pl.when(j % chunks == chunks - 1)
        def _():
            if rest < width:
                buffer = (gate_w, up_w, down_w)[kind]
                shape = (width - rest, buffer.shape[2])
                buffer[j % WEIGHT_SLOTS, rest:, :] = jnp.zeros(shape, jnp.bfloat16)
            weight_copy(kind, j, rest).start()

    def loaded(kind, j):
        @pl.when(j % chunks < chunks - 1)
        def _():
            weight_copy(kind, j, width).wait()

        @pl.when(j % chunks == chunks - 1)
        def _():
            weight_copy(kind, j, rest).wait()

    def exchange(s, j):
        slot = j % slots
        size = width >> (s + 1)
        if s == 0:
            at = pl.multiple_of((1 - bits[0]) * size, size)
            source = product.at[slot, :, pl.ds(at, size), :]
        else:
            source = outgoing[s].at[slot]
        return pltpu.make_async_remote_copy(
            src_ref=source,
            dst_ref=received[s].at[slot],
            send_sem=send_sem.at[s, slot],
            recv_sem=recv_sem.at[s, slot],
            device_id=(partner_of(s, j), my_col),
            device_id_type=MESH,
        )

    def gather(i, j):
        slot = j % hidden_slots
        size = block << i
        at = pl.ds(pl.multiple_of(by_turn(places, j) // (1 << i) * size, size), size)
        return pltpu.make_async_remote_copy(
            src_ref=hidden.at[slot, at, :],
            dst_ref=hidden.at[slot, at, :],
            send_sem=gather_send.at[i, slot],
            recv_sem=gather_recv.at[i, slot],
            device_id=(partner_of(k - 1 - i, j), my_col),
            device_id_type=MESH,
        )

    def rows_of(s, j, first, size):
        slot = j % slots
        if s == 1:
            at = pl.multiple_of(bits[0] * (width >> 1) + first, size)
            mine = product[slot, :, pl.ds(at, size), :]
        else:
            mine = kept[s - 1][slot, :, pl.ds(first, size), :]
        return mine + received[s - 1][slot, :, pl.ds(first, size), :].astype(jnp.float32)

    def halve(s, j):
        size = width >> (s + 1)
        slot = j % slots
        bit = bit_of(s, j)
        away = pl.multiple_of((1 - bit) * size, size)
        stay = pl.multiple_of(bit * size, size)
        exchange(s - 1, j).wait()
        outgoing[s][slot] = rows_of(s, j, away, size).astype(jnp.bfloat16)
        exchange(s, j).start()
        kept[s][slot] = rows_of(s, j, stay, size)

    def activate(j):
        exchange(k - 1, j).wait()
        sums = rows_of(k, j, 0, block)
        gate, up = sums[0], sums[1]
        at = pl.multiple_of(by_turn(places, j) * block, block)
        value = (gate / (1.0 + jnp.exp(-gate)) * up).astype(jnp.bfloat16)
        hidden[j % hidden_slots, pl.ds(at, block), :] = value
        gather(0, j).start()

    def spread(i, j):
        gather(i - 1, j).wait_recv()
        gather(i, j).start()

    def down(j):
        gather(k - 1, j).wait_recv()
        loaded(2, j)
        units = (((0,), (0,)), ((), ()))
        total[j // chunks] += lax.dot_general(
            hidden[j % hidden_slots],
            down_w[j % WEIGHT_SLOTS],
            units,
            preferred_element_type=jnp.float32,
        )
        for i in range(k):
            gather(i, j).wait_send()

    def project(j):
        slot = j % slots
        loaded(0, j)
        loaded(1, j)
        x = x_ref[j // chunks]
        product[slot, 0] = jnp.dot(
            gate_w[j % WEIGHT_SLOTS], x, preferred_element_type=jnp.float32
        )
        product[slot, 1] = jnp.dot(up_w[j % WEIGHT_SLOTS], x, preferred_element_type=jnp.float32)
        exchange(0, j).start()

    steps = [project]
    steps += [functools.partial(halve, s) for s in range(1, k)]
    steps += [activate]
    steps += [functools.partial(spread, i) for i in range(1, k)]
    steps += [down]
    last = len(steps) - 1

    pieces = own.shape[1]
    deep = blocks_ref.shape[1]
    behind = [my_col, cols - 1 - my_col]
    line_steps = pieces + 2 * (cols - 1)

    def block_copy(step):
        other = (me + step) % n
        return pltpu.make_async_remote_copy(
            src_ref=blocks_ref.at[other],
            dst_ref=plane.at[pl.ds(pl.multiple_of(me * deep, deep), deep), :],
            send_sem=block_send.at[step - 1],
            recv_sem=block_recv.at[step - 1],
            device_id=(other, my_col),
            device_id_type=MESH,
        )

    def line_copy(batch, way, f):
        return pltpu.make_async_remote_copy(
            src_ref=line_out.at[batch, way, f],
            dst_ref=line_in.at[batch, way, f],
            send_sem=line_send.at[batch, way, f],
            recv_sem=line_recv.at[batch, way, f],
            device_id=(me, (my_col + (1 if way == 0 else cols - 1)) % cols),
            device_id_type=MESH,
        )

    def place_rows():
        count = lengths_ref.shape[1]
        f32 = jnp.float32
        lengths = lengths_ref[...].astype(f32)
        prefix = prefix_ref[...].astype(f32)
        owner = owner_ref[...]
        down_id = lax.broadcasted_iota(jnp.int32, (count, count), 0)
        over_id = lax.broadcasted_iota(jnp.int32, (count, count), 1)
        same = down_id == over_id
        lengths_down = jnp.sum(jnp.where(same, lengths, 0.0), axis=1, keepdims=True)
        prefix_down = jnp.sum(jnp.where(same, prefix, 0.0), axis=1, keepdims=True)
        before = (prefix_down > prefix) | ((prefix_down == prefix) & (down_id < over_id))
        starts = jnp.sum(jnp.where(before, lengths_down, 0.0), axis=0, keepdims=True)
        first = (owner // cols * deep).astype(f32) - starts
        first = jnp.where(owner % cols == my_col, first, -1e6)
        row = lax.broadcasted_iota(jnp.int32, (batches * tokens, 1), 0)
        batch, at = row // tokens, row % tokens
        token = ((at // part * batches + batch) * part + at % part).astype(f32)
        inside = (token >= starts) & (token < starts + lengths)
        return token + jnp.sum(jnp.where(inside, first, 0.0), axis=1, keepdims=True)

    def pick(batch, place):
        column = lax.broadcasted_iota(jnp.int32, (tokens, n * deep), 1).astype(jnp.float32)
        for side in range(2):
            chosen = (column == place + float(side * (deep // 2))).astype(jnp.bfloat16)
            rows = jnp.dot(chosen, plane[...], preferred_element_type=jnp.float32)
            rows = rows.astype(jnp.bfloat16)
            for f in range(pieces // 2):
                own[batch, side * (pieces // 2) + f] = rows[:, f * PIECE : (f + 1) * PIECE]

    def pass_on(batch, u):
        for way in range(2):
            f = u - 2 * behind[way]

            @pl.when((f >= 0) & (f < pieces))
            def _():
                @pl.when(behind[way] > 0)
                def _():
                    line_copy(batch, way, f).wait_recv()

                @pl.when(behind[way] < cols - 1)
                def _():
                    line_out[batch, way, f] = own[batch, f] + line_in[batch, way, f]
                    line_copy(batch, way, f).start()

    def join(batch):
        for f in range(pieces):
            at = slice(f * PIECE, (f + 1) * PIECE)
            rows = own[batch, f] + line_in[batch, 0, f] + line_in[batch, 1, f]
            x_ref[batch, at, :] = rows.T

    def col_copy(batch, step):
        return pltpu.make_async_remote_copy(
            src_ref=col_out.at[batch, step - 1],
            dst_ref=col_in.at[batch, step - 1],
            send_sem=col_send.at[batch, step - 1],
            recv_sem=col_recv.at[batch, step - 1],
            device_id=(me, (my_col + step) % cols),
            device_id_type=MESH,
        )

    def send_cols(batch):
        for step in range(1, cols):
            other = (my_col + step) % cols
            rows = total[batch, pl.ds(pl.multiple_of(other * part, part), part), :]
            col_out[batch, step - 1] = rows.astype(jnp.bfloat16)
            col_copy(batch, step).start()

    for step in range(1, n):
        block_copy(step).start()
    ahead = WEIGHT_SLOTS - 1
    for j in range(min(ahead, every)):
        for kind in range(3):
            load(kind, jnp.int32(j))
    plane[pl.ds(pl.multiple_of(me * deep, deep), deep), :] = blocks_ref[me]
    total[...] = jnp.zeros_like(total)
    for way in range(2):
        @pl.when(behind[way] == 0)
        def _():
            for batch in range(batches):
                line_in[batch, way] = jnp.zeros(line_in.shape[2:], jnp.bfloat16)

    place = place_rows()
    for step in range(1, n):
        block_copy(step).wait()
    for batch in range(batches):
        pick(batch, place[batch * tokens : (batch + 1) * tokens])

    def first_line(u, carry):
        pass_on(0, u)
        return carry

    lax.fori_loop(0, line_steps, first_line, 0)
    join(0)
    per_round = -(-line_steps // chunks)

    def round_of(t, carry):
        @pl.when(t + ahead < every)
        def _():
            load(0, t + ahead)
            load(1, t + ahead)

        j_down = t - last * LAG + ahead

        @pl.when((j_down >= ahead) & (j_down < every))
        def _():
            load(2, j_down)

        for batch in range(1, batches):
            @pl.when(t == batch * chunks)
            def _():
                join(batch)

        for s in range(last, -1, -1):
            j = t - s * LAG

            @pl.when((j >= 0) & (j < every))
            def _():
                steps[s](j)

        for batch in range(1, batches):
            for q in range(per_round):
                pass_on(batch, (t - (batch - 1) * chunks) * per_round + q)

        for batch in range(batches):
            @pl.when(t == (batch + 1) * chunks - 1 + last * LAG)
            def _():
                send_cols(batch)

        return carry

    lax.fori_loop(0, every + last * LAG, round_of, 0)

    for batch in range(batches):
        for way in range(2):
            @pl.when(behind[way] < cols - 1)
            def _():
                for f in range(pieces):
                    line_copy(batch, way, f).wait_send()

    for batch in range(batches):
        result = total[batch, pl.ds(pl.multiple_of(my_col * part, part), part), :]
        for step in range(1, cols):
            col_copy(batch, step).wait()
            result = result + col_in[batch, step - 1].astype(jnp.float32)
        out_ref[batch * part : (batch + 1) * part, :] = result.astype(jnp.bfloat16)


def on_device(
    owned_rows, suffix_lengths, owner_map, prefix_lengths, gate_weight, up_weight, down_weight
):
    n, cols = lax.axis_size("row"), lax.axis_size("col")
    slot_size = owned_rows.shape[0]
    all_tokens = TOK_DEV * suffix_lengths.shape[0]
    depth, units = gate_weight.shape
    out_width = down_weight.shape[1]
    deep = 2 * slot_size
    blocks = owned_rows.reshape(slot_size, n, 2, depth // 2).transpose(1, 2, 0, 3)
    blocks = blocks.reshape(n, deep, depth // 2)

    width, batches = CHUNK, BATCHES
    tokens = all_tokens // batches
    chunks = -(-units // width)
    k = n.bit_length() - 1
    slots, hidden_slots = 2 * LAG, (k + 1) * LAG
    part = tokens // cols
    pieces = depth // PIECE
    bf16, f32 = jnp.bfloat16, jnp.float32
    dma = pltpu.SemaphoreType.DMA
    scratch = [
        pltpu.VMEM((slots, 2, width, tokens), f32),
        pltpu.VMEM((hidden_slots, width, tokens), bf16),
        pltpu.VMEM((batches, tokens, out_width), f32),
        pltpu.VMEM((WEIGHT_SLOTS, width, depth), bf16),
        pltpu.VMEM((WEIGHT_SLOTS, width, depth), bf16),
        pltpu.VMEM((WEIGHT_SLOTS, width, out_width), bf16),
        pltpu.VMEM((batches, cols - 1, part, out_width), bf16),
        pltpu.VMEM((batches, cols - 1, part, out_width), bf16),
        pltpu.VMEM((batches, depth, tokens), bf16),
        pltpu.VMEM((n * deep, depth // 2), bf16),
        pltpu.VMEM((batches, pieces, tokens, PIECE), bf16),
        pltpu.VMEM((batches, 2, pieces, tokens, PIECE), bf16),
        pltpu.VMEM((batches, 2, pieces, tokens, PIECE), bf16),
        dma((k, slots)),
        dma((k, slots)),
        dma((k, hidden_slots)),
        dma((k, hidden_slots)),
        dma((3, WEIGHT_SLOTS)),
        dma((batches, cols - 1)),
        dma((batches, cols - 1)),
        dma((n - 1,)),
        dma((n - 1,)),
        dma((batches, 2, pieces)),
        dma((batches, 2, pieces)),
    ]
    sizes = [width >> (s + 1) for s in range(k)]
    scratch += [
        pltpu.VMEM((slots, 2, size, tokens), f32 if s == 0 else bf16)
        for s, size in enumerate(sizes)
    ]
    scratch += [pltpu.VMEM((slots, 2, size, tokens), bf16) for size in sizes[1:]]
    scratch += [pltpu.VMEM((slots, 2, size, tokens), f32) for size in sizes[1:]]
    vmem = pl.BlockSpec(memory_space=pltpu.VMEM)
    hbm = pl.BlockSpec(memory_space=pl.ANY)
    return pl.pallas_call(
        functools.partial(layer_kernel, n, cols, chunks, batches),
        out_shape=jax.ShapeDtypeStruct((batches * part, out_width), bf16),
        in_specs=[vmem] * 4 + [hbm] * 3,
        out_specs=vmem,
        scratch_shapes=scratch,
        compiler_params=pltpu.CompilerParams(
            collective_id=0, has_side_effects=True, vmem_limit_bytes=56 * 1024 * 1024
        ),
        cost_estimate=pl.CostEstimate(
            flops=6 * all_tokens * depth * units,
            bytes_accessed=6 * depth * units * batches,
            transcendentals=all_tokens * units // n,
        ),
    )(
        suffix_lengths[None],
        owner_map[None],
        prefix_lengths[None],
        blocks,
        gate_weight.T,
        up_weight.T,
        down_weight,
    )


def solution(mesh):
    return jax.shard_map(
        on_device,
        mesh=mesh,
        in_specs=(
            P(("row", "col"), None),
            P(),
            P(),
            P(),
            P("row", "col"),
            P("row", "col"),
            P("col", "row"),
        ),
        out_specs=P("col", "row"),
        check_vma=False,
    )
```

```python
import functools

import jax
import jax.numpy as jnp
from jax import lax
from jax.experimental import pallas as pl
from jax.experimental.pallas import tpu as pltpu
from jax.sharding import PartitionSpec as P

TOK_DEV = 8
CHUNK = 512
BATCHES = 2
WEIGHT_SLOTS = 4
PIECE = 128
MESH = pl.DeviceIdType.MESH


def layer_kernel(
    n, cols, chunks, batches, lag,
    lengths_ref, owner_ref, prefix_ref, owned_ref, gate_ref, up_ref, down_ref, out_ref,
    product, hidden, total, gate_w, up_w, down_w, col_out, col_in,
    x_ref, blocks_ref, plane, own, line_out, line_in,
    send_sem, recv_sem, gather_send, gather_recv, weight_sem, col_send, col_recv,
    block_send, block_recv, line_send, line_recv, *stages,
):
    k = n.bit_length() - 1
    width, tokens = CHUNK, x_ref.shape[2]
    every = batches * chunks
    rest = gate_ref.shape[0] - (chunks - 1) * width
    block = width >> k
    part = tokens // cols
    slots, near_slots, hidden_slots = 2 * lag, lag + 1, (k + 1) * lag
    received = stages[:k]
    outgoing = (None,) + stages[k : 2 * k - 1]
    kept = (None,) + stages[2 * k - 1 :]

    me = lax.axis_index("row")
    my_col = lax.axis_index("col")
    bits = [(me // (1 << b)) % 2 for b in range(k)]
    partners = [me + (1 - 2 * bits[b]) * (1 << b) for b in range(k)]
    orders = [list(range(k)), [0] + list(range(k - 1, 0, -1))]
    places = [sum(bits[b] * (1 << (k - 1 - i)) for i, b in enumerate(order)) for order in orders]

    def by_turn(values, j):
        return values[0] + (j % 2) * (values[1] - values[0])

    def bit_of(s, j):
        return by_turn([bits[order[s]] for order in orders], j)

    def partner_of(s, j):
        return by_turn([partners[order[s]] for order in orders], j)

    barrier = pltpu.get_barrier_semaphore()
    for step in range(1, n):
        other = (me + step) % n
        pl.semaphore_signal(barrier, inc=1, device_id=(other, my_col), device_id_type=MESH)
    for step in range(1, cols):
        other = (my_col + step) % cols
        pl.semaphore_signal(barrier, inc=1, device_id=(me, other), device_id_type=MESH)
    side_width = blocks_ref.shape[2]
    for r in range(n):
        sides = [
            owned_ref[:, (2 * r + side) * side_width : (2 * r + side + 1) * side_width]
            for side in range(2)
        ]
        both = jnp.concatenate([side.astype(jnp.float32) for side in sides], axis=0)
        blocks_ref[r] = both.astype(jnp.bfloat16)
    pl.semaphore_wait(barrier, n - 1 + cols - 1)

    def weight_copy(kind, j, rows):
        array, buffer = ((gate_ref, gate_w), (up_ref, up_w), (down_ref, down_w))[kind]
        slot = j % WEIGHT_SLOTS
        first = pl.multiple_of(j % chunks * width, width)
        return pltpu.make_async_copy(
            array.at[pl.ds(first, rows), :],
            buffer.at[slot, pl.ds(0, rows), :],
            weight_sem.at[kind, slot],
        )

    def load(kind, j):
        @pl.when(j % chunks < chunks - 1)
        def _():
            weight_copy(kind, j, width).start()

        @pl.when(j % chunks == chunks - 1)
        def _():
            if rest < width:
                buffer = (gate_w, up_w, down_w)[kind]
                shape = (width - rest, buffer.shape[2])
                buffer[j % WEIGHT_SLOTS, rest:, :] = jnp.zeros(shape, jnp.bfloat16)
            weight_copy(kind, j, rest).start()

    def loaded(kind, j):
        @pl.when(j % chunks < chunks - 1)
        def _():
            weight_copy(kind, j, width).wait()

        @pl.when(j % chunks == chunks - 1)
        def _():
            weight_copy(kind, j, rest).wait()

    def exchange(s, j):
        slot = j % slots
        size = width >> (s + 1)
        if s == 0:
            at = pl.multiple_of((1 - bits[0]) * size, size)
            source = product.at[j % near_slots, :, pl.ds(at, size), :]
        else:
            source = outgoing[s].at[j % near_slots]
        return pltpu.make_async_remote_copy(
            src_ref=source,
            dst_ref=received[s].at[slot],
            send_sem=send_sem.at[s, slot],
            recv_sem=recv_sem.at[s, slot],
            device_id=(partner_of(s, j), my_col),
            device_id_type=MESH,
        )

    def gather(i, j):
        slot = j % hidden_slots
        size = block << i
        at = pl.ds(pl.multiple_of(by_turn(places, j) // (1 << i) * size, size), size)
        return pltpu.make_async_remote_copy(
            src_ref=hidden.at[slot, at, :],
            dst_ref=hidden.at[slot, at, :],
            send_sem=gather_send.at[i, slot],
            recv_sem=gather_recv.at[i, slot],
            device_id=(partner_of(k - 1 - i, j), my_col),
            device_id_type=MESH,
        )

    def rows_of(s, j, first, size):
        slot = j % slots
        if s == 1:
            at = pl.multiple_of(bits[0] * (width >> 1) + first, size)
            mine = product[j % near_slots, :, pl.ds(at, size), :]
        else:
            mine = kept[s - 1][j % near_slots, :, pl.ds(first, size), :]
        return mine + received[s - 1][slot, :, pl.ds(first, size), :].astype(jnp.float32)

    def halve(s, j):
        size = width >> (s + 1)
        slot = j % near_slots
        bit = bit_of(s, j)
        away = pl.multiple_of((1 - bit) * size, size)
        stay = pl.multiple_of(bit * size, size)
        exchange(s - 1, j).wait()
        outgoing[s][slot] = rows_of(s, j, away, size).astype(jnp.bfloat16)
        exchange(s, j).start()
        kept[s][slot] = rows_of(s, j, stay, size)

    def activate(j):
        exchange(k - 1, j).wait()
        sums = rows_of(k, j, 0, block)
        gate, up = sums[0], sums[1]
        at = pl.multiple_of(by_turn(places, j) * block, block)
        value = (gate / (1.0 + jnp.exp(-gate)) * up).astype(jnp.bfloat16)
        hidden[j % hidden_slots, pl.ds(at, block), :] = value
        gather(0, j).start()

    def spread(i, j):
        gather(i - 1, j).wait_recv()
        gather(i, j).start()

    def down(j):
        gather(k - 1, j).wait_recv()
        loaded(2, j)
        units = (((0,), (0,)), ((), ()))
        total[j // chunks] += lax.dot_general(
            hidden[j % hidden_slots],
            down_w[j % WEIGHT_SLOTS],
            units,
            preferred_element_type=jnp.float32,
        )
        for i in range(k):
            gather(i, j).wait_send()

    def project(j):
        slot = j % near_slots
        loaded(0, j)
        loaded(1, j)
        x = x_ref[j // chunks]
        product[slot, 0] = jnp.dot(
            gate_w[j % WEIGHT_SLOTS], x, preferred_element_type=jnp.float32
        )
        product[slot, 1] = jnp.dot(up_w[j % WEIGHT_SLOTS], x, preferred_element_type=jnp.float32)
        exchange(0, j).start()

    steps = [project]
    steps += [functools.partial(halve, s) for s in range(1, k)]
    steps += [activate]
    steps += [functools.partial(spread, i) for i in range(1, k)]
    steps += [down]
    last = len(steps) - 1

    pieces = own.shape[1]
    deep = blocks_ref.shape[1]
    behind = [my_col, cols - 1 - my_col]
    line_steps = pieces + 2 * (cols - 1)

    def block_copy(step):
        other = (me + step) % n
        return pltpu.make_async_remote_copy(
            src_ref=blocks_ref.at[other],
            dst_ref=plane.at[pl.ds(pl.multiple_of(me * deep, deep), deep), :],
            send_sem=block_send.at[step - 1],
            recv_sem=block_recv.at[step - 1],
            device_id=(other, my_col),
            device_id_type=MESH,
        )

    def line_copy(batch, way, f):
        return pltpu.make_async_remote_copy(
            src_ref=line_out.at[batch, way, f],
            dst_ref=line_in.at[batch, way, f],
            send_sem=line_send.at[batch, way, f],
            recv_sem=line_recv.at[batch, way, f],
            device_id=(me, (my_col + (1 if way == 0 else cols - 1)) % cols),
            device_id_type=MESH,
        )

    def place_rows():
        count = lengths_ref.shape[1]
        f32 = jnp.float32
        lengths = lengths_ref[...].astype(f32)
        prefix = prefix_ref[...].astype(f32)
        owner = owner_ref[...]
        down_id = lax.broadcasted_iota(jnp.int32, (count, count), 0)
        over_id = lax.broadcasted_iota(jnp.int32, (count, count), 1)
        same = down_id == over_id
        lengths_down = jnp.sum(jnp.where(same, lengths, 0.0), axis=1, keepdims=True)
        prefix_down = jnp.sum(jnp.where(same, prefix, 0.0), axis=1, keepdims=True)
        before = (prefix_down > prefix) | ((prefix_down == prefix) & (down_id < over_id))
        starts = jnp.sum(jnp.where(before, lengths_down, 0.0), axis=0, keepdims=True)
        first = (owner // cols * deep).astype(f32) - starts
        first = jnp.where(owner % cols == my_col, first, -1e6)
        row = lax.broadcasted_iota(jnp.int32, (batches * tokens, 1), 0)
        batch, at = row // tokens, row % tokens
        token = ((at // part * batches + batch) * part + at % part).astype(f32)
        inside = (token >= starts) & (token < starts + lengths)
        return token + jnp.sum(jnp.where(inside, first, 0.0), axis=1, keepdims=True)

    def pick(batch, place):
        column = lax.broadcasted_iota(jnp.int32, (tokens, n * deep), 1).astype(jnp.float32)
        for side in range(2):
            chosen = (column == place + float(side * (deep // 2))).astype(jnp.bfloat16)
            rows = jnp.dot(chosen, plane[...], preferred_element_type=jnp.float32)
            rows = rows.astype(jnp.bfloat16)
            for f in range(pieces // 2):
                own[batch, side * (pieces // 2) + f] = rows[:, f * PIECE : (f + 1) * PIECE]

    def pass_on(batch, u):
        for way in range(2):
            f = u - 2 * behind[way]

            @pl.when((f >= 0) & (f < pieces))
            def _():
                @pl.when(behind[way] > 0)
                def _():
                    line_copy(batch, way, f).wait_recv()

                @pl.when(behind[way] < cols - 1)
                def _():
                    line_out[batch, way, f] = own[batch, f] + line_in[batch, way, f]
                    line_copy(batch, way, f).start()

    def join(batch):
        for f in range(pieces):
            at = slice(f * PIECE, (f + 1) * PIECE)
            rows = own[batch, f] + line_in[batch, 0, f] + line_in[batch, 1, f]
            x_ref[batch, at, :] = rows.T

    def col_copy(batch, step):
        return pltpu.make_async_remote_copy(
            src_ref=col_out.at[batch, step - 1],
            dst_ref=col_in.at[batch, step - 1],
            send_sem=col_send.at[batch, step - 1],
            recv_sem=col_recv.at[batch, step - 1],
            device_id=(me, (my_col + step) % cols),
            device_id_type=MESH,
        )

    def send_cols(batch):
        for step in range(1, cols):
            other = (my_col + step) % cols
            rows = total[batch, pl.ds(pl.multiple_of(other * part, part), part), :]
            col_out[batch, step - 1] = rows.astype(jnp.bfloat16)
            col_copy(batch, step).start()

    for step in range(1, n):
        block_copy(step).start()
    ahead = WEIGHT_SLOTS - 1
    for j in range(min(ahead, every)):
        for kind in range(3):
            load(kind, jnp.int32(j))
    plane[pl.ds(pl.multiple_of(me * deep, deep), deep), :] = blocks_ref[me]
    total[...] = jnp.zeros_like(total)
    for way in range(2):
        @pl.when(behind[way] == 0)
        def _():
            for batch in range(batches):
                line_in[batch, way] = jnp.zeros(line_in.shape[2:], jnp.bfloat16)

    place = place_rows()
    for step in range(1, n):
        block_copy(step).wait()
    for batch in range(batches):
        pick(batch, place[batch * tokens : (batch + 1) * tokens])

    def first_line(u, carry):
        pass_on(0, u)
        return carry

    lax.fori_loop(0, line_steps, first_line, 0)
    join(0)
    per_round = -(-line_steps // chunks)

    def round_of(t, carry):
        @pl.when(t + ahead < every)
        def _():
            load(0, t + ahead)
            load(1, t + ahead)

        j_down = t - last * lag + ahead

        @pl.when((j_down >= ahead) & (j_down < every))
        def _():
            load(2, j_down)

        for batch in range(1, batches):
            @pl.when(t == batch * chunks)
            def _():
                join(batch)

        for s in range(last, -1, -1):
            j = t - s * lag

            @pl.when((j >= 0) & (j < every))
            def _():
                steps[s](j)

        for batch in range(1, batches):
            for q in range(per_round):
                pass_on(batch, (t - (batch - 1) * chunks) * per_round + q)

        for batch in range(batches):
            @pl.when(t == (batch + 1) * chunks - 1 + last * lag)
            def _():
                send_cols(batch)

        return carry

    lax.fori_loop(0, every + last * lag, round_of, 0)

    for batch in range(batches):
        for way in range(2):
            @pl.when(behind[way] < cols - 1)
            def _():
                for f in range(pieces):
                    line_copy(batch, way, f).wait_send()

    for batch in range(batches):
        result = total[batch, pl.ds(pl.multiple_of(my_col * part, part), part), :]
        for step in range(1, cols):
            col_copy(batch, step).wait()
            result = result + col_in[batch, step - 1].astype(jnp.float32)
        out_ref[batch * part : (batch + 1) * part, :] = result.astype(jnp.bfloat16)


def on_device(
    owned_rows, suffix_lengths, owner_map, prefix_lengths, gate_weight, up_weight, down_weight
):
    n, cols = lax.axis_size("row"), lax.axis_size("col")
    slot_size = owned_rows.shape[0]
    all_tokens = TOK_DEV * suffix_lengths.shape[0]
    depth, units = gate_weight.shape
    out_width = down_weight.shape[1]
    deep = 2 * slot_size

    width, batches = CHUNK, BATCHES
    tokens = all_tokens // batches
    chunks = -(-units // width)
    k = n.bit_length() - 1
    lag = 4 if tokens * width <= 1 << 16 else 2
    slots, near_slots, hidden_slots = 2 * lag, lag + 1, (k + 1) * lag
    part = tokens // cols
    pieces = depth // PIECE
    bf16, f32 = jnp.bfloat16, jnp.float32
    dma = pltpu.SemaphoreType.DMA
    scratch = [
        pltpu.VMEM((near_slots, 2, width, tokens), f32),
        pltpu.VMEM((hidden_slots, width, tokens), bf16),
        pltpu.VMEM((batches, tokens, out_width), f32),
        pltpu.VMEM((WEIGHT_SLOTS, width, depth), bf16),
        pltpu.VMEM((WEIGHT_SLOTS, width, depth), bf16),
        pltpu.VMEM((WEIGHT_SLOTS, width, out_width), bf16),
        pltpu.VMEM((batches, cols - 1, part, out_width), bf16),
        pltpu.VMEM((batches, cols - 1, part, out_width), bf16),
        pltpu.VMEM((batches, depth, tokens), bf16),
        pltpu.VMEM((n, deep, depth // 2), bf16),
        pltpu.VMEM((n * deep, depth // 2), bf16),
        pltpu.VMEM((batches, pieces, tokens, PIECE), bf16),
        pltpu.VMEM((batches, 2, pieces, tokens, PIECE), bf16),
        pltpu.VMEM((batches, 2, pieces, tokens, PIECE), bf16),
        dma((k, slots)),
        dma((k, slots)),
        dma((k, hidden_slots)),
        dma((k, hidden_slots)),
        dma((3, WEIGHT_SLOTS)),
        dma((batches, cols - 1)),
        dma((batches, cols - 1)),
        dma((n - 1,)),
        dma((n - 1,)),
        dma((batches, 2, pieces)),
        dma((batches, 2, pieces)),
    ]
    sizes = [width >> (s + 1) for s in range(k)]
    scratch += [
        pltpu.VMEM((slots, 2, size, tokens), f32 if s == 0 else bf16)
        for s, size in enumerate(sizes)
    ]
    scratch += [pltpu.VMEM((near_slots, 2, size, tokens), bf16) for size in sizes[1:]]
    scratch += [pltpu.VMEM((near_slots, 2, size, tokens), f32) for size in sizes[1:]]
    vmem = pl.BlockSpec(memory_space=pltpu.VMEM)
    hbm = pl.BlockSpec(memory_space=pl.ANY)
    return pl.pallas_call(
        functools.partial(layer_kernel, n, cols, chunks, batches, lag),
        out_shape=jax.ShapeDtypeStruct((batches * part, out_width), bf16),
        in_specs=[vmem] * 4 + [hbm] * 3,
        out_specs=vmem,
        scratch_shapes=scratch,
        compiler_params=pltpu.CompilerParams(
            collective_id=0, has_side_effects=True, vmem_limit_bytes=56 * 1024 * 1024
        ),
        cost_estimate=pl.CostEstimate(
            flops=6 * all_tokens * depth * units,
            bytes_accessed=6 * depth * units * batches,
            transcendentals=all_tokens * units // n,
        ),
    )(
        suffix_lengths[None],
        owner_map[None],
        prefix_lengths[None],
        owned_rows,
        gate_weight.T,
        up_weight.T,
        down_weight,
    )


def solution(mesh):
    return jax.shard_map(
        on_device,
        mesh=mesh,
        in_specs=(
            P(("row", "col"), None),
            P(),
            P(),
            P(),
            P("row", "col"),
            P("row", "col"),
            P("col", "row"),
        ),
        out_specs=P("col", "row"),
        check_vma=False,
    )
```

```python
import functools

import jax
import jax.numpy as jnp
from jax import lax
from jax.experimental import pallas as pl
from jax.experimental.pallas import tpu as pltpu
from jax.sharding import PartitionSpec as P

TOK_DEV = 8
CHUNK = 512
BATCHES = 2
WEIGHT_SLOTS = 4
PIECE = 128
MESH = pl.DeviceIdType.MESH


def layer_kernel(
    n, cols, chunks, batches, lag,
    lengths_ref, owner_ref, prefix_ref, owned_ref, gate_ref, up_ref, down_ref, out_ref,
    product, hidden, total, gate_w, up_w, down_w, col_out, col_in,
    x_ref, blocks_ref, plane, own, line_out, line_in,
    send_sem, recv_sem, gather_send, gather_recv, weight_sem, col_send, col_recv,
    block_send, block_recv, line_send, line_recv, *stages,
):
    k = n.bit_length() - 1
    width, tokens = CHUNK, x_ref.shape[2]
    every = batches * chunks
    rest = gate_ref.shape[0] - (chunks - 1) * width
    block = width >> k
    part = tokens // cols
    slots, near_slots, hidden_slots = 2 * lag, lag + 1, (k + 1) * lag
    received = stages[:k]
    outgoing = (None,) + stages[k : 2 * k - 1]
    kept = (None,) + stages[2 * k - 1 :]

    me = lax.axis_index("row")
    my_col = lax.axis_index("col")
    bits = [(me // (1 << b)) % 2 for b in range(k)]
    partners = [me + (1 - 2 * bits[b]) * (1 << b) for b in range(k)]
    orders = [list(range(k)), [0] + list(range(k - 1, 0, -1))]
    places = [sum(bits[b] * (1 << (k - 1 - i)) for i, b in enumerate(order)) for order in orders]

    def by_turn(values, j):
        return values[0] + (j % 2) * (values[1] - values[0])

    def bit_of(s, j):
        return by_turn([bits[order[s]] for order in orders], j)

    def partner_of(s, j):
        return by_turn([partners[order[s]] for order in orders], j)

    barrier = pltpu.get_barrier_semaphore()
    for step in range(1, n):
        other = (me + step) % n
        pl.semaphore_signal(barrier, inc=1, device_id=(other, my_col), device_id_type=MESH)
    for step in range(1, cols):
        other = (my_col + step) % cols
        pl.semaphore_signal(barrier, inc=1, device_id=(me, other), device_id_type=MESH)
    side_width = blocks_ref.shape[2]
    for r in range(n):
        sides = [
            owned_ref[:, (2 * r + side) * side_width : (2 * r + side + 1) * side_width]
            for side in range(2)
        ]
        both = jnp.concatenate([side.astype(jnp.float32) for side in sides], axis=0)
        blocks_ref[r] = both.astype(jnp.bfloat16)
    pl.semaphore_wait(barrier, n - 1 + cols - 1)

    def weight_copy(kind, j, rows):
        array, buffer = ((gate_ref, gate_w), (up_ref, up_w), (down_ref, down_w))[kind]
        slot = j % WEIGHT_SLOTS
        first = pl.multiple_of(j % chunks * width, width)
        return pltpu.make_async_copy(
            array.at[pl.ds(first, rows), :],
            buffer.at[slot, pl.ds(0, rows), :],
            weight_sem.at[kind, slot],
        )

    def load(kind, j):
        @pl.when(j % chunks < chunks - 1)
        def _():
            weight_copy(kind, j, width).start()

        @pl.when(j % chunks == chunks - 1)
        def _():
            if rest < width:
                buffer = (gate_w, up_w, down_w)[kind]
                shape = (width - rest, buffer.shape[2])
                buffer[j % WEIGHT_SLOTS, rest:, :] = jnp.zeros(shape, jnp.bfloat16)
            weight_copy(kind, j, rest).start()

    def loaded(kind, j):
        @pl.when(j % chunks < chunks - 1)
        def _():
            weight_copy(kind, j, width).wait()

        @pl.when(j % chunks == chunks - 1)
        def _():
            weight_copy(kind, j, rest).wait()

    def exchange(s, j):
        slot = j % slots
        size = width >> (s + 1)
        if s == 0:
            at = pl.multiple_of((1 - bits[0]) * size, size)
            source = product.at[j % near_slots, :, pl.ds(at, size), :]
        else:
            source = outgoing[s].at[j % near_slots]
        return pltpu.make_async_remote_copy(
            src_ref=source,
            dst_ref=received[s].at[slot],
            send_sem=send_sem.at[s, slot],
            recv_sem=recv_sem.at[s, slot],
            device_id=(partner_of(s, j), my_col),
            device_id_type=MESH,
        )

    def gather(i, j):
        slot = j % hidden_slots
        size = block << i
        at = pl.ds(pl.multiple_of(by_turn(places, j) // (1 << i) * size, size), size)
        return pltpu.make_async_remote_copy(
            src_ref=hidden.at[slot, at, :],
            dst_ref=hidden.at[slot, at, :],
            send_sem=gather_send.at[i, slot],
            recv_sem=gather_recv.at[i, slot],
            device_id=(partner_of(k - 1 - i, j), my_col),
            device_id_type=MESH,
        )

    def rows_of(s, j, first, size):
        slot = j % slots
        if s == 1:
            at = pl.multiple_of(bits[0] * (width >> 1) + first, size)
            mine = product[j % near_slots, :, pl.ds(at, size), :]
        else:
            mine = kept[s - 1][j % near_slots, :, pl.ds(first, size), :]
        return mine + received[s - 1][slot, :, pl.ds(first, size), :].astype(jnp.float32)

    def halve(s, j):
        size = width >> (s + 1)
        slot = j % near_slots
        bit = bit_of(s, j)
        away = pl.multiple_of((1 - bit) * size, size)
        stay = pl.multiple_of(bit * size, size)
        exchange(s - 1, j).wait()
        outgoing[s][slot] = rows_of(s, j, away, size).astype(jnp.bfloat16)
        exchange(s, j).start()
        kept[s][slot] = rows_of(s, j, stay, size)

    def activate(j):
        exchange(k - 1, j).wait()
        sums = rows_of(k, j, 0, block)
        gate, up = sums[0], sums[1]
        at = pl.multiple_of(by_turn(places, j) * block, block)
        value = (gate / (1.0 + jnp.exp(-gate)) * up).astype(jnp.bfloat16)
        hidden[j % hidden_slots, pl.ds(at, block), :] = value
        gather(0, j).start()

    def spread(i, j):
        gather(i - 1, j).wait_recv()
        gather(i, j).start()

    def down(j):
        gather(k - 1, j).wait_recv()
        loaded(2, j)
        units = (((0,), (0,)), ((), ()))
        total[j // chunks] += lax.dot_general(
            hidden[j % hidden_slots],
            down_w[j % WEIGHT_SLOTS],
            units,
            preferred_element_type=jnp.float32,
        )
        for i in range(k):
            gather(i, j).wait_send()

    def project(j):
        slot = j % near_slots
        loaded(0, j)
        loaded(1, j)
        x = x_ref[j // chunks]
        product[slot, 0] = jnp.dot(
            gate_w[j % WEIGHT_SLOTS], x, preferred_element_type=jnp.float32
        )
        product[slot, 1] = jnp.dot(up_w[j % WEIGHT_SLOTS], x, preferred_element_type=jnp.float32)
        exchange(0, j).start()

    steps = [project]
    steps += [functools.partial(halve, s) for s in range(1, k)]
    steps += [activate]
    steps += [functools.partial(spread, i) for i in range(1, k)]
    steps += [down]
    last = len(steps) - 1

    pieces = own.shape[1]
    deep = blocks_ref.shape[1]
    behind = [my_col, cols - 1 - my_col]
    hop, late_hop = 2, 6

    def block_copy(step):
        other = (me + step) % n
        return pltpu.make_async_remote_copy(
            src_ref=blocks_ref.at[other],
            dst_ref=plane.at[pl.ds(pl.multiple_of(me * deep, deep), deep), :],
            send_sem=block_send.at[step - 1],
            recv_sem=block_recv.at[step - 1],
            device_id=(other, my_col),
            device_id_type=MESH,
        )

    def line_copy(batch, way, f):
        return pltpu.make_async_remote_copy(
            src_ref=line_out.at[batch, way, f],
            dst_ref=line_in.at[batch, way, f],
            send_sem=line_send.at[batch, way, f],
            recv_sem=line_recv.at[batch, way, f],
            device_id=(me, (my_col + (1 if way == 0 else cols - 1)) % cols),
            device_id_type=MESH,
        )

    def place_rows():
        count = lengths_ref.shape[1]
        f32 = jnp.float32
        lengths = lengths_ref[...].astype(f32)
        prefix = prefix_ref[...].astype(f32)
        owner = owner_ref[...]
        down_id = lax.broadcasted_iota(jnp.int32, (count, count), 0)
        over_id = lax.broadcasted_iota(jnp.int32, (count, count), 1)
        same = down_id == over_id
        lengths_down = jnp.sum(jnp.where(same, lengths, 0.0), axis=1, keepdims=True)
        prefix_down = jnp.sum(jnp.where(same, prefix, 0.0), axis=1, keepdims=True)
        before = (prefix_down > prefix) | ((prefix_down == prefix) & (down_id < over_id))
        starts = jnp.sum(jnp.where(before, lengths_down, 0.0), axis=0, keepdims=True)
        first = (owner // cols * deep).astype(f32) - starts
        first = jnp.where(owner % cols == my_col, first, -1e6)
        row = lax.broadcasted_iota(jnp.int32, (batches * tokens, 1), 0)
        batch, at = row // tokens, row % tokens
        token = ((at // part * batches + batch) * part + at % part).astype(f32)
        inside = (token >= starts) & (token < starts + lengths)
        return token + jnp.sum(jnp.where(inside, first, 0.0), axis=1, keepdims=True)

    def pick(batch, place):
        column = lax.broadcasted_iota(jnp.int32, (tokens, n * deep), 1).astype(jnp.float32)
        for side in range(2):
            chosen = (column == place + float(side * (deep // 2))).astype(jnp.bfloat16)
            rows = jnp.dot(chosen, plane[...], preferred_element_type=jnp.float32)
            rows = rows.astype(jnp.bfloat16)
            for f in range(pieces // 2):
                own[batch, side * (pieces // 2) + f] = rows[:, f * PIECE : (f + 1) * PIECE]

    def pass_on(batch, u):
        for way in range(2):
            f = u - (hop if batch == 0 else late_hop) * behind[way]

            @pl.when((f >= 0) & (f < pieces))
            def _():
                @pl.when(behind[way] > 0)
                def _():
                    line_copy(batch, way, f).wait_recv()

                @pl.when(behind[way] < cols - 1)
                def _():
                    line_out[batch, way, f] = own[batch, f] + line_in[batch, way, f]
                    line_copy(batch, way, f).start()

    def join(batch):
        for f in range(pieces):
            at = slice(f * PIECE, (f + 1) * PIECE)
            rows = own[batch, f] + line_in[batch, 0, f] + line_in[batch, 1, f]
            x_ref[batch, at, :] = rows.T

    def col_copy(batch, step):
        return pltpu.make_async_remote_copy(
            src_ref=col_out.at[batch, step - 1],
            dst_ref=col_in.at[batch, step - 1],
            send_sem=col_send.at[batch, step - 1],
            recv_sem=col_recv.at[batch, step - 1],
            device_id=(me, (my_col + step) % cols),
            device_id_type=MESH,
        )

    def send_cols(batch):
        for step in range(1, cols):
            other = (my_col + step) % cols
            rows = total[batch, pl.ds(pl.multiple_of(other * part, part), part), :]
            col_out[batch, step - 1] = rows.astype(jnp.bfloat16)
            col_copy(batch, step).start()

    for step in range(1, n):
        block_copy(step).start()
    ahead = WEIGHT_SLOTS - 1
    for j in range(min(ahead, every)):
        for kind in range(3):
            load(kind, jnp.int32(j))
    plane[pl.ds(pl.multiple_of(me * deep, deep), deep), :] = blocks_ref[me]
    total[...] = jnp.zeros_like(total)
    for way in range(2):
        @pl.when(behind[way] == 0)
        def _():
            for batch in range(batches):
                line_in[batch, way] = jnp.zeros(line_in.shape[2:], jnp.bfloat16)

    place = place_rows()
    for step in range(1, n):
        block_copy(step).wait()
    pick(0, place[:tokens])

    def first_line(u, carry):
        pass_on(0, u)
        return carry

    lax.fori_loop(0, pieces + hop * (cols - 1), first_line, 0)
    join(0)
    per_round = -(-(pieces + late_hop * (cols - 1)) // chunks)

    def round_of(t, carry):
        @pl.when(t + ahead < every)
        def _():
            load(0, t + ahead)
            load(1, t + ahead)

        j_down = t - last * lag + ahead

        @pl.when((j_down >= ahead) & (j_down < every))
        def _():
            load(2, j_down)

        for batch in range(1, batches):
            @pl.when(t == batch * chunks)
            def _():
                join(batch)

        for s in range(last, -1, -1):
            j = t - s * lag

            @pl.when((j >= 0) & (j < every))
            def _():
                steps[s](j)

        for batch in range(1, batches):
            @pl.when(t == (batch - 1) * chunks)
            def _():
                pick(batch, place[batch * tokens : (batch + 1) * tokens])

            for q in range(per_round):
                pass_on(batch, (t - (batch - 1) * chunks) * per_round + q)

        for batch in range(batches):
            @pl.when(t == (batch + 1) * chunks - 1 + last * lag)
            def _():
                send_cols(batch)

        return carry

    lax.fori_loop(0, every + last * lag, round_of, 0)

    for batch in range(batches):
        for way in range(2):
            @pl.when(behind[way] < cols - 1)
            def _():
                for f in range(pieces):
                    line_copy(batch, way, f).wait_send()

    for batch in range(batches):
        result = total[batch, pl.ds(pl.multiple_of(my_col * part, part), part), :]
        for step in range(1, cols):
            col_copy(batch, step).wait()
            result = result + col_in[batch, step - 1].astype(jnp.float32)
        out_ref[batch * part : (batch + 1) * part, :] = result.astype(jnp.bfloat16)


def on_device(
    owned_rows, suffix_lengths, owner_map, prefix_lengths, gate_weight, up_weight, down_weight
):
    n, cols = lax.axis_size("row"), lax.axis_size("col")
    slot_size = owned_rows.shape[0]
    all_tokens = TOK_DEV * suffix_lengths.shape[0]
    depth, units = gate_weight.shape
    out_width = down_weight.shape[1]
    deep = 2 * slot_size

    width, batches = CHUNK, BATCHES
    tokens = all_tokens // batches
    chunks = -(-units // width)
    k = n.bit_length() - 1
    lag = 4 if tokens * width <= 1 << 16 else 2
    slots, near_slots, hidden_slots = 2 * lag, lag + 1, (k + 1) * lag
    part = tokens // cols
    pieces = depth // PIECE
    bf16, f32 = jnp.bfloat16, jnp.float32
    dma = pltpu.SemaphoreType.DMA
    scratch = [
        pltpu.VMEM((near_slots, 2, width, tokens), f32),
        pltpu.VMEM((hidden_slots, width, tokens), bf16),
        pltpu.VMEM((batches, tokens, out_width), f32),
        pltpu.VMEM((WEIGHT_SLOTS, width, depth), bf16),
        pltpu.VMEM((WEIGHT_SLOTS, width, depth), bf16),
        pltpu.VMEM((WEIGHT_SLOTS, width, out_width), bf16),
        pltpu.VMEM((batches, cols - 1, part, out_width), bf16),
        pltpu.VMEM((batches, cols - 1, part, out_width), bf16),
        pltpu.VMEM((batches, depth, tokens), bf16),
        pltpu.VMEM((n, deep, depth // 2), bf16),
        pltpu.VMEM((n * deep, depth // 2), bf16),
        pltpu.VMEM((batches, pieces, tokens, PIECE), bf16),
        pltpu.VMEM((batches, 2, pieces, tokens, PIECE), bf16),
        pltpu.VMEM((batches, 2, pieces, tokens, PIECE), bf16),
        dma((k, slots)),
        dma((k, slots)),
        dma((k, hidden_slots)),
        dma((k, hidden_slots)),
        dma((3, WEIGHT_SLOTS)),
        dma((batches, cols - 1)),
        dma((batches, cols - 1)),
        dma((n - 1,)),
        dma((n - 1,)),
        dma((batches, 2, pieces)),
        dma((batches, 2, pieces)),
    ]
    sizes = [width >> (s + 1) for s in range(k)]
    scratch += [
        pltpu.VMEM((slots, 2, size, tokens), f32 if s == 0 else bf16)
        for s, size in enumerate(sizes)
    ]
    scratch += [pltpu.VMEM((near_slots, 2, size, tokens), bf16) for size in sizes[1:]]
    scratch += [pltpu.VMEM((near_slots, 2, size, tokens), f32) for size in sizes[1:]]
    vmem = pl.BlockSpec(memory_space=pltpu.VMEM)
    hbm = pl.BlockSpec(memory_space=pl.ANY)
    return pl.pallas_call(
        functools.partial(layer_kernel, n, cols, chunks, batches, lag),
        out_shape=jax.ShapeDtypeStruct((batches * part, out_width), bf16),
        in_specs=[vmem] * 4 + [hbm] * 3,
        out_specs=vmem,
        scratch_shapes=scratch,
        compiler_params=pltpu.CompilerParams(
            collective_id=0, has_side_effects=True, vmem_limit_bytes=56 * 1024 * 1024
        ),
        cost_estimate=pl.CostEstimate(
            flops=6 * all_tokens * depth * units,
            bytes_accessed=6 * depth * units * batches,
            transcendentals=all_tokens * units // n,
        ),
    )(
        suffix_lengths[None],
        owner_map[None],
        prefix_lengths[None],
        owned_rows,
        gate_weight.T,
        up_weight.T,
        down_weight,
    )


def solution(mesh):
    return jax.shard_map(
        on_device,
        mesh=mesh,
        in_specs=(
            P(("row", "col"), None),
            P(),
            P(),
            P(),
            P("row", "col"),
            P("row", "col"),
            P("col", "row"),
        ),
        out_specs=P("col", "row"),
        check_vma=False,
    )
```
